32 devices in a mesh: section: 2 (over core), expert: 4 (over z), dp: 4 (over y, x).
Axes of the slice: x: 2, y: 2, z: 4, core: 2. Of those that a mesh axis runs over, the one named last changes fastest.
Arguments:
- tokens: bfloat16 [2048, 768], P(('expert', 'dp')), may hold values from -6 to 6
- cotangent: bfloat16 [2, 2048, 768], P('section', ('expert', 'dp')), may hold values from -6 to 6
- qkv_weight: bfloat16 [2, 3, 768, 768], P('section', None, ('expert', 'dp')), may hold values from -0.21875 to 0.21875
- out_weight: bfloat16 [2, 768, 768], P('section', ('expert', 'dp')), may hold values from -0.625 to 0.625
- norm_gains: bfloat16 [2, 2, 768], P('section', None, ('expert', 'dp')), may hold values from 0.099609375 to 1.8984375
- router_weight: bfloat16 [2, 768, 4], P('section', ('expert', 'dp')), may hold values from -0.21875 to 0.21875
- bias_table: bfloat16 [2, 32, 12], P('section'), may hold values from -4 to 4
- expert_in: bfloat16 [2, 4, 768, 3072], P('section', 'expert', None, 'dp'), may hold values from -0.21875 to 0.21875
- expert_out: bfloat16 [2, 4, 3072, 768], P('section', 'expert', 'dp'), may hold values from -1.75 to 1.75
- routes: int32 [2, 2048, 1], P('section', ('expert', 'dp')), may hold values from 0 to 3; in each aligned block of 64 rows (0 to 63, 64 to 127, ..., all dimensions but the last counted through in order) at most 21 rows name the same one
Outputs:
- hidden_states: bfloat16 [2, 2048, 768], P('section', ('expert', 'dp'))
- input_grads: float32 [2, 2048, 768], P('section', ('expert', 'dp'))
- qkv_grad: float32 [2, 3, 768, 768], P('section', None, ('expert', 'dp'))
- out_grad: float32 [2, 768, 768], P('section', ('expert', 'dp'))
- gains_grad: float32 [2, 2, 768], P('section', None, ('expert', 'dp'))
- router_grad: float32 [2, 768, 4], P('section', ('expert', 'dp'))
- table_grad: float32 [2, 32, 12], P('section')
- expert_in_grad: float32 [2, 4, 768, 3072], P('section', 'expert', None, 'dp')
- expert_out_grad: float32 [2, 4, 3072, 768], P('section', 'expert', 'dp')
The draws below stay inside these ranges and needn't reach their ends.
Inputs may be any that keep to these rules, and one draw needn't show every extreme that they name: `routes`: in each aligned block of 64 rows (one sequence) no expert is named by more than 21 rows, a bound that some block reaches.
All inputs are finite; a program needn't handle non-finite values.
Results may differ from the reference program's by a relative error of at most 0.028.
Values may be sent and summed in bfloat16 or wider, within the bound.
A program may use at most 192 MiB of HBM per device.

```python
import math
import jax
import jax.numpy as jnp
import numpy as np
from jax import lax

D = 768
HEADS = 12
HEAD_DIM = 64
FF = 3072
BUCKETS = 32
SEQ = 64
MB = 2
EXPERTS = 4
CAP = 21
TOKENS = 2048
N_SECTION = 2
N_EXPERT = 4
N_DP = 4


def block_levels(rng, shape, cuts, smallest, high):
    factor_of, own = 1.0, jax.random.fold_in(rng, 6)
    for position, parts in cuts:
        steps = jnp.exp(jax.random.uniform(jax.random.fold_in(own, position), (parts,), jnp.float32, smallest / len(cuts), high / len(cuts)))
        factor_of = factor_of * jnp.repeat(steps, shape[position] // parts).reshape([-1 if axis == position else 1 for axis in range(len(shape))])
    return factor_of


def routed_block(own_key, own, number, rows, number_of, top, reach, lean):
    order = jax.random.permutation(own_key, number_of)
    heavy_load, usual = load_shares(number_of, rows * top, reach, lean, True), load_shares(number_of, rows * top, reach, lean, False)
    places = jnp.arange(number_of)

    def named(lengths, turn):
        used = int((lengths > 0).sum())
        fixed = max(1, used // 4)
        passed = fixed + (places - fixed + turn * (used - fixed)) % max(1, number_of - fixed)
        return jnp.zeros((number_of,), jnp.int32).at[order[jnp.where(places < fixed, places, passed)]].set(jnp.asarray(lengths, jnp.int32))

    lengths = jnp.where(number % 4 == 0, named(heavy_load, number // 4), named(usual, number - number // 4 - 1))
    mixed = jax.random.permutation(jax.random.fold_in(own, 3), number_of)
    donor, taker = mixed[0:number_of // 2 * 2:2], mixed[1:number_of // 2 * 2:2]
    slack = jnp.minimum(lengths[donor] - 1, reach - lengths[taker]) // 2
    slack = jnp.where((donor == order[0]) | (taker == order[0]) | (lengths[taker] == 0), 0, jnp.maximum(slack, 0))
    passed = jax.random.randint(jax.random.fold_in(own, 4), (number_of // 2,), 0, 1 << 20) % (slack + 1)
    lengths = lengths.at[donor].add(-passed).at[taker].add(passed)
    members = jnp.searchsorted(jnp.cumsum(lengths), jnp.arange(rows * top), side="right").astype(jnp.int32)
    listing = members.reshape(top, rows).T
    listing = listing[jax.random.permutation(jax.random.fold_in(own, 1), rows)]
    turn = jax.random.randint(jax.random.fold_in(own, 2), (rows, 1), 0, top)
    return jnp.take_along_axis(listing, (jnp.arange(top)[None, :] + turn) % top, axis=1)


def load_shares(amount, total, limit, skew, full):
    loads = [(1 << 20) // math.isqrt(standing ** skew) + 1 for standing in range(1, amount + 1)]
    largest = limit if full else min(limit, max(-(-total // amount), total * loads[0] // sum(loads)))
    least = 1 if total - largest >= amount - 1 else 0
    holding, surplus = [largest] + [least] * (amount - 1), total - largest - least * (amount - 1)
    while surplus > 0:
        movable = [i for i in range(1, amount) if holding[i] < largest] or [i for i in range(1, amount) if holding[i] < limit]
        pool, remaining = sum([loads[i] for i in movable]), surplus
        for i in movable:
            more = min(limit - holding[i], max(1, remaining * loads[i] // pool), surplus)
            holding[i] = holding[i] + more
            surplus = surplus - more
    return np.array(holding)


def normal_values(stream_key, extent, deviation, limit, cuts=(), kind=jnp.bfloat16):
    level = block_levels(stream_key, extent, cuts, -0.22, 0.18) if cuts else 1.0
    drawn = jax.random.normal(stream_key, extent, jnp.float32) * deviation * level
    return jnp.minimum(jnp.maximum(drawn, -limit), limit).astype(kind)


def setup_inputs(seed: int = 0) -> dict:
    streams_of = jax.random.split(jax.random.key(seed), 11)
    tokens = normal_values(streams_of[0], (TOKENS, D), 1.0, 6.0, ((0, 16),))
    cotangent = normal_values(streams_of[1], (N_SECTION, TOKENS, D), 1.0, 6.0, ((0, 2), (1, 16)))
    qkv_weight = normal_values(streams_of[2], (N_SECTION, 3, D, D), D ** -0.5, 0.21875, ((0, 2), (2, 16)))
    out_weight = normal_values(streams_of[3], (N_SECTION, D, D), (D // 8) ** -0.5, 0.625, ((0, 2), (1, 16)))
    norm_gains = jnp.clip(1.0 + 0.18 * jax.random.normal(streams_of[4], (N_SECTION, 2, D), jnp.float32), 0.099609375, 1.8984375).astype(jnp.bfloat16)
    router_weight = normal_values(streams_of[5], (N_SECTION, D, EXPERTS), D ** -0.5, 0.21875, ((0, 2), (1, 16)))
    bias_table = normal_values(streams_of[6], (N_SECTION, BUCKETS, HEADS), 1.0, 4.0, ((0, 2),))
    expert_in = normal_values(streams_of[7], (N_SECTION, EXPERTS, D, FF), D ** -0.5, 0.21875, ((0, 2), (1, 4), (3, 4)))
    expert_out = normal_values(streams_of[8], (N_SECTION, EXPERTS, FF, D), (max(1, FF // 256)) ** -0.5, 1.75, ((0, 2), (1, 4), (2, 4)))
    routes_keys = jax.random.split(jax.random.fold_in(streams_of[9], 1), N_SECTION * TOKENS // SEQ)
    routes_turns = jax.random.permutation(jax.random.fold_in(streams_of[9], 3), N_SECTION * TOKENS // SEQ)
    routes = jax.vmap(lambda own, number: routed_block(jax.random.fold_in(streams_of[9], 2), own, number, SEQ, EXPERTS, 1, CAP, 2))(routes_keys, routes_turns).reshape((N_SECTION, TOKENS, 1))
    return {"tokens": tokens, "cotangent": cotangent, "qkv_weight": qkv_weight, "out_weight": out_weight, "norm_gains": norm_gains, "router_weight": router_weight, "bias_table": bias_table, "expert_in": expert_in, "expert_out": expert_out, "routes": routes}


HIGHEST_PRECISION = lax.Precision.HIGHEST
EPSILON = 1e-06
BUCKET_EDGES = (12, 16, 23, 32, 46, 64, 91)

@jax.custom_vjp
def low(v):
    return lax.optimization_barrier(v.astype(jnp.bfloat16)).astype(jnp.float32)

@jax.custom_vjp
def low_back(v):
    return v

def low_keep(v):
    return (low(v), None)

def low_pass(kept, grad):
    return (grad,)

def back_keep(v):
    return (v, None)

def back_low(kept, grad):
    return (low(grad),)
low.defvjp(low_keep, low_pass)
low_back.defvjp(back_keep, back_low)

def bucket_grid(length):
    places = jnp.arange(length, dtype=jnp.int32)
    offset = places[None, :] - places[:, None]
    distance = jnp.abs(offset)
    far_bucket = 8 + sum(((distance >= edge).astype(jnp.int32) for edge in BUCKET_EDGES))
    near_far = jnp.where(distance < 8, distance, far_bucket)
    return near_far + 16 * (offset > 0).astype(jnp.int32)

def slot_positions(route_now, experts):
    route_hot = (route_now[..., None] == jnp.arange(experts, dtype=jnp.int32)).astype(jnp.int32)
    before = jnp.cumsum(route_hot, axis=-2) - route_hot
    return lax.optimization_barrier(jnp.sum(before * route_hot, axis=-1))

def rms_norm(values, gain):
    return values * lax.rsqrt(lax.optimization_barrier(jnp.mean(values * values, axis=-1, keepdims=True)) + EPSILON) * gain

def switch_layer(source, weights, route_now, bucket_map):
    qkv_w, out_w, gains, router_w, table, w_in, w_out = weights
    groups, length, model_width = source.shape
    experts = w_in.shape[0]
    normed_a = low(rms_norm(source, gains[0]))
    qkv = low_back(low(jnp.einsum('gnd,cde->cgne', normed_a, qkv_w, precision=HIGHEST_PRECISION)))
    split = qkv.reshape(3, groups, length, HEADS, HEAD_DIM)
    bucket_hot = (bucket_map[..., None] == jnp.arange(BUCKETS, dtype=jnp.int32)).astype(jnp.float32)
    bias_heads = jnp.einsum('qkb,bh->hqk', bucket_hot, table, precision=HIGHEST_PRECISION)
    scores = jnp.einsum('gqhe,gkhe->ghqk', split[0], split[1], precision=HIGHEST_PRECISION) * HEAD_DIM ** (-0.5)
    scores = low_back(scores + bias_heads[None])
    probs = low(jax.nn.softmax(scores, axis=-1))
    mixed_heads = jnp.einsum('ghqk,gkhe->gqhe', probs, split[2], precision=HIGHEST_PRECISION)
    mixed_heads = low_back(low(mixed_heads.reshape(groups, length, model_width)))
    hidden = source + low_back(jnp.einsum('gnd,de->gne', mixed_heads, out_w, precision=HIGHEST_PRECISION))
    normed_b = low(rms_norm(hidden, gains[1]))
    logits = jnp.einsum('gnd,de->gne', normed_b, router_w, precision=HIGHEST_PRECISION)
    route_hot = (route_now[..., None] == jnp.arange(experts, dtype=jnp.int32)).astype(jnp.float32)
    gate_prob = lax.optimization_barrier(jnp.sum(jax.nn.softmax(logits, axis=-1) * route_hot, axis=-1))
    slot_cell = route_now * CAP + slot_positions(route_now, experts)
    sending = (slot_cell[:, None, :] == jnp.arange(experts * CAP, dtype=jnp.int32)[None, :, None]).astype(jnp.float32)
    buffer = jnp.einsum('gcn,gnd->gcd', sending, low_back(normed_b), precision=HIGHEST_PRECISION)
    buffer = buffer.reshape(groups, experts, CAP, model_width).transpose(1, 0, 2, 3).reshape(experts, groups * CAP, model_width)
    inner_pre = low_back(jnp.einsum('erd,edf->erf', buffer, w_in, precision=HIGHEST_PRECISION))
    active = low(jax.nn.gelu(inner_pre, approximate=True))
    result = low_back(low(jnp.einsum('erf,efd->erd', active, w_out, precision=HIGHEST_PRECISION)))
    result = result.reshape(experts, groups, CAP, model_width).transpose(1, 0, 2, 3).reshape(groups, experts * CAP, model_width)
    combined = jnp.einsum('gcn,gcd->gnd', sending, result, precision=HIGHEST_PRECISION)
    return hidden + gate_prob[..., None] * combined

def section_pair(source, extra, weights, route_pair, bucket_map):
    first = tuple((member[0] for member in weights))
    second = tuple((member[1] for member in weights))
    layer_one = switch_layer(source, first, route_pair[0], bucket_map)
    layer_two = switch_layer(low(layer_one) + extra, second, route_pair[1], bucket_map)
    return (layer_one, layer_two)

def reference(tokens, cotangent, qkv_weight, out_weight, norm_gains, router_weight, bias_table, expert_in, expert_out, routes):
    weights = tuple((member.astype(jnp.float32) for member in (qkv_weight, out_weight, norm_gains, router_weight, bias_table, expert_in, expert_out)))
    group_shape = (N_EXPERT, N_DP * MB, SEQ, D)
    source = tokens.astype(jnp.float32).reshape(group_shape)
    extra = jnp.zeros(group_shape, jnp.float32)
    route_groups = routes[..., 0].reshape(N_SECTION, N_EXPERT, N_DP * MB, SEQ).transpose(1, 0, 2, 3)
    bucket_map = bucket_grid(SEQ)

    def forward(source_all, extra_all, weight_all):

        def group_pass(group_item):
            return section_pair(group_item[0], group_item[1], weight_all, group_item[2], bucket_map)
        return lax.map(jax.checkpoint(group_pass), (source_all, extra_all, route_groups))
    (layer_one, layer_two), pull = jax.vjp(forward, source, extra, weights)
    grad_in = (cotangent[0].astype(jnp.float32).reshape(group_shape), cotangent[1].astype(jnp.float32).reshape(group_shape))
    grad_source, grad_extra, grad_weights = pull(grad_in)
    hidden_states = jnp.stack([layer_one.reshape(-1, D), layer_two.reshape(-1, D)]).astype(jnp.bfloat16)
    input_grads = jnp.stack([grad_source.reshape(-1, D), grad_extra.reshape(-1, D)])
    return (hidden_states, input_grads, grad_weights[0], grad_weights[1], grad_weights[2], grad_weights[3], grad_weights[4], grad_weights[5], grad_weights[6])
```

```python
from functools import partial

import jax
import jax.numpy as jnp
from jax import lax
from jax.experimental import pallas as pl
from jax.experimental.pallas import tpu as pltpu
from jax.sharding import PartitionSpec as P

BUCKETS = 32
SEQ = 64


EPSILON = 1e-06
BUCKET_EDGES = (12, 16, 23, 32, 46, 64, 91)


def passed_along(value, axis, steps):
    count = lax.axis_size(axis)
    first, last = (max(0, -steps), min(count, count - steps))
    return lax.ppermute(value, axis, [(source, source + steps) for source in range(first, last)])


def bucket_grid(length):
    places = jnp.arange(length, dtype=jnp.int32)
    offset = places[None, :] - places[:, None]
    distance = jnp.abs(offset)
    far_bucket = 8 + sum(((distance >= edge).astype(jnp.int32) for edge in BUCKET_EDGES))
    near_far = jnp.where(distance < 8, distance, far_bucket)
    return near_far + 16 * (offset > 0).astype(jnp.int32)


def slot_positions(route_now, experts):
    route_hot = (route_now[..., None] == jnp.arange(experts, dtype=jnp.int32)).astype(jnp.int32)
    before = jnp.cumsum(route_hot, axis=-2) - route_hot
    return jnp.sum(before * route_hot, axis=-1)


def rms_norm(values, gain):
    return values * lax.rsqrt(jnp.mean(values * values, axis=-1, keepdims=True) + EPSILON) * gain


def gelu_tanh(values):
    return jax.nn.gelu(values, approximate=True)


def gate_of(route_hot, logits):
    return jnp.sum(jax.nn.softmax(logits, axis=-1) * route_hot, axis=-1)


def split_heads(flat, head_count):
    return flat.reshape(flat.shape[0] // SEQ, SEQ, head_count, -1).transpose(0, 2, 1, 3)


def join_heads(split):
    return split.transpose(0, 2, 1, 3).reshape(split.shape[0] * SEQ, -1)


MESH = pl.DeviceIdType.MESH
VMEM_LIMIT = 56 * 1024 * 1024


def at_group(e, d):
    return {"expert": e, "dp": d}


def greet(peers):
    barrier = pltpu.get_barrier_semaphore()
    for peer in peers:
        pl.semaphore_signal(barrier, inc=1, device_id=peer, device_id_type=MESH)
    pl.semaphore_wait(barrier, len(peers))


def remote(src, dst, send_sem, recv_sem, peer):
    return pltpu.make_async_remote_copy(
        src_ref=src, dst_ref=dst, send_sem=send_sem, recv_sem=recv_sem,
        device_id=peer, device_id_type=MESH,
    )


def group_peers(ne, nd):
    e, d = lax.axis_index("expert"), lax.axis_index("dp")
    return [
        (lax.rem(e + ke, ne), lax.rem(d + kd, nd))
        for ke in range(ne) for kd in range(nd) if ke or kd
    ]


def gather_kernel(ne, nd, shard, full, send_sem, recv_sem, own_sem):
    e, d = lax.axis_index("expert"), lax.axis_index("dp")
    along_e = [lax.rem(e + k, ne) for k in range(1, ne)]
    along_d = [lax.rem(d + k, nd) for k in range(1, nd)]
    greet([at_group(pe, d) for pe in along_e] + [at_group(e, pd) for pd in along_d])
    me = e * nd + d
    own = pltpu.make_async_copy(shard, full.at[me], own_sem)
    own.start()
    sent = []
    for pe in along_e:
        copy = remote(shard, full.at[me], send_sem.at[len(sent)], recv_sem.at[me], at_group(pe, d))
        copy.start()
        sent.append(copy)
    for pd in along_d:
        copy = remote(shard, full.at[me], send_sem.at[len(sent)], recv_sem.at[me], at_group(e, pd))
        copy.start()
        sent.append(copy)
    for pe in along_e:
        slot = pe * nd + d
        remote(shard, full.at[slot], send_sem.at[0], recv_sem.at[slot], at_group(pe, d)).wait_recv()
        for pd in along_d:
            copy = remote(
                full.at[slot], full.at[slot], send_sem.at[len(sent)], recv_sem.at[slot],
                at_group(e, pd),
            )
            copy.start()
            sent.append(copy)
    for ke in range(ne):
        for pd in along_d:
            slot = lax.rem(e + ke, ne) * nd + pd
            remote(shard, full.at[slot], send_sem.at[0], recv_sem.at[slot], at_group(e, pd)).wait_recv()
    for copy in sent:
        copy.wait_send()
    own.wait()


def gather_shards(shard, ne, nd, ident):
    groups = ne * nd
    return pl.pallas_call(
        partial(gather_kernel, ne, nd),
        out_shape=jax.ShapeDtypeStruct((groups,) + shard.shape, shard.dtype),
        in_specs=[pl.BlockSpec(memory_space=pl.ANY)],
        out_specs=pl.BlockSpec(memory_space=pl.ANY),
        scratch_shapes=[
            pltpu.SemaphoreType.DMA((ne - 1 + ne * (nd - 1),)),
            pltpu.SemaphoreType.DMA((groups,)),
            pltpu.SemaphoreType.DMA,
        ],
        compiler_params=pltpu.CompilerParams(collective_id=ident, has_side_effects=True),
        name="gather_weights",
    )(shard)


def reduce_kernel(
    ne, nd, section, parts, total, first, staged, second,
    send_a, recv_a, send_b, recv_b, own_sem,
):
    @pl.when(lax.axis_index("section") == section)
    def _():
        e, d = lax.axis_index("expert"), lax.axis_index("dp")
        order_e = [lax.rem(e + k, ne) for k in range(1, ne + 1)]
        along_d = [lax.rem(d + k, nd) for k in range(1, nd)]
        greet([at_group(pe, d) for pe in order_e[:-1]] + [at_group(e, pd) for pd in along_d])
        own = pltpu.make_async_copy
        sent, kept = [], []
        for i, pe in enumerate(order_e):
            copy = own(parts.at[pe * nd + d], first.at[d, pe], own_sem.at[i])
            copy.start()
            kept.append(copy)
            for pd in along_d:
                copy = remote(
                    parts.at[pe * nd + pd], first.at[d, pe],
                    send_a.at[len(sent)], recv_a.at[d, pe], at_group(e, pd),
                )
                copy.start()
                sent.append(copy)
        sent_b = []
        for i, pe in enumerate(order_e):
            kept[i].wait()
            for pd in along_d:
                remote(
                    parts.at[0], first.at[pd, pe], send_a.at[0], recv_a.at[pd, pe], at_group(e, pd)
                ).wait_recv()
            value = first[0, pe].astype(jnp.float32)
            for j in range(1, nd):
                value = value + first[j, pe].astype(jnp.float32)
            value = value.astype(jnp.bfloat16)
            if i < ne - 1:
                staged[i] = value
                copy = remote(
                    staged.at[i], second.at[e], send_b.at[i], recv_b.at[e], at_group(pe, d)
                )
                copy.start()
                sent_b.append(copy)
            else:
                second[e] = value
        for pe in order_e[:-1]:
            remote(
                staged.at[0], second.at[pe], send_b.at[0], recv_b.at[pe], at_group(pe, d)
            ).wait_recv()
        value = second[0].astype(jnp.float32)
        for j in range(1, ne):
            value = value + second[j].astype(jnp.float32)
        total[...] = value
        for copy in sent + sent_b:
            copy.wait_send()


def reduce_parts(parts, ne, nd, section, ident):
    rows, width = parts.shape[1:]
    dma = pltpu.SemaphoreType.DMA
    return pl.pallas_call(
        partial(reduce_kernel, ne, nd, section),
        out_shape=jax.ShapeDtypeStruct((rows, width), jnp.float32),
        in_specs=[pl.BlockSpec(memory_space=pl.ANY)],
        out_specs=pl.BlockSpec(memory_space=pltpu.VMEM),
        scratch_shapes=[
            pltpu.VMEM((nd, ne, rows, width), jnp.bfloat16),
            pltpu.VMEM((ne - 1, rows, width), jnp.bfloat16),
            pltpu.VMEM((ne, rows, width), jnp.bfloat16),
            dma((ne * (nd - 1),)), dma((nd, ne)), dma((ne - 1,)), dma((ne,)), dma((ne,)),
        ],
        compiler_params=pltpu.CompilerParams(
            collective_id=ident, has_side_effects=True, vmem_limit_bytes=VMEM_LIMIT
        ),
        name="reduce_grads",
    )(parts)


def exchange(ne, nd, rows_out, arrived, staged, returned, sems, work):
    send_a, recv_a, send_b, recv_b = sems
    e, d = lax.axis_index("expert"), lax.axis_index("dp")
    me = e * nd + d
    peers = group_peers(ne, nd)
    greet([at_group(*peer) for peer in peers])
    out_a = []
    for i, (pe, pd) in enumerate(peers):
        copy = remote(
            rows_out.at[pe], arrived.at[me], send_a.at[i], recv_a.at[me], at_group(pe, pd)
        )
        copy.start()
        out_a.append(copy)
    arrived[me] = rows_out[e]
    out_b = []
    for ke in range(ne):
        pe = lax.rem(e + ne - ke, ne)
        for kd in range(nd):
            if ke or kd:
                pd = lax.rem(d + nd - kd, nd)
                slot = pe * nd + pd
                remote(
                    rows_out.at[0], arrived.at[slot], send_a.at[0], recv_a.at[slot],
                    at_group(pe, pd),
                ).wait_recv()
        work(pe)
        for kd in range(nd):
            pd = lax.rem(d + nd - kd, nd)
            slot = pe * nd + pd
            if ke or kd:
                copy = remote(
                    staged.at[slot], returned.at[me], send_b.at[len(out_b)], recv_b.at[me],
                    at_group(pe, pd),
                )
                copy.start()
                out_b.append(copy)
            else:
                returned[me] = staged[slot]
    for pe, pd in peers:
        slot = pe * nd + pd
        remote(
            staged.at[slot], returned.at[slot], send_b.at[0], recv_b.at[slot], at_group(pe, pd)
        ).wait_recv()
    for copy in out_a + out_b:
        copy.wait_send()


def moe_forward_kernel(
    ne, nd, section, rows_out, w_in, w_out, arrived, pre, returned, staged, *sems
):
    slots, width = rows_out.shape[1:]

    def work(pe):
        block = pl.ds(pe * nd, nd)
        rows = arrived[block].reshape(nd * slots, width)
        inner = jnp.dot(rows, w_in[...], preferred_element_type=jnp.float32)
        pre[block] = inner.reshape(nd, slots, -1)
        act = gelu_tanh(inner).astype(jnp.bfloat16)
        part = jnp.dot(act, w_out[...], preferred_element_type=jnp.float32)
        staged[block] = part.astype(jnp.bfloat16).reshape(nd, slots, width)

    @pl.when(lax.axis_index("section") == section)
    def _():
        exchange(ne, nd, rows_out, arrived, staged, returned, sems, work)


def moe_backward_kernel(
    ne, nd, section, rows_out, pre, w_in, w_out, arrived, inner_grad, act, returned, staged, *sems
):
    slots, width = rows_out.shape[1:]
    turned = (((1,), (1,)), ((), ()))

    def work(pe):
        block = pl.ds(pe * nd, nd)
        rows = arrived[block].reshape(nd * slots, width)
        grad_act = lax.dot_general(rows, w_out[...], turned, preferred_element_type=jnp.float32)
        u = pre[block].reshape(nd * slots, -1)
        square = u * u
        bend = jnp.tanh(0.7978845608028654 * (u + 0.044715 * square * u))
        act[block] = (0.5 * u * (1.0 + bend)).astype(jnp.bfloat16).reshape(nd, slots, -1)
        slope = 0.5 * (1.0 + bend) + 0.5 * u * (1.0 - bend * bend) * (
            0.7978845608028654 * (1.0 + 3 * 0.044715 * square)
        )
        grad = (grad_act * slope).astype(jnp.bfloat16)
        inner_grad[block] = grad.reshape(nd, slots, -1)
        part = lax.dot_general(grad, w_in[...], turned, preferred_element_type=jnp.float32)
        staged[block] = part.astype(jnp.bfloat16).reshape(nd, slots, width)

    @pl.when(lax.axis_index("section") == section)
    def _():
        exchange(ne, nd, rows_out, arrived, staged, returned, sems, work)


def moe_call(kernel, operands, outs, ne, nd, section, ident, name):
    groups = ne * nd
    slots, width = operands[0].shape[1:]
    dma = pltpu.SemaphoreType.DMA
    vmem = pl.BlockSpec(memory_space=pltpu.VMEM)
    return pl.pallas_call(
        partial(kernel, ne, nd, section),
        out_shape=[jax.ShapeDtypeStruct((groups, slots, w), t) for w, t in outs],
        in_specs=[vmem] * len(operands),
        out_specs=[vmem] * len(outs),
        scratch_shapes=[
            pltpu.VMEM((groups, slots, width), jnp.bfloat16),
            dma((groups - 1,)), dma((groups,)), dma((groups - 1,)), dma((groups,)),
        ],
        compiler_params=pltpu.CompilerParams(
            collective_id=ident, has_side_effects=True, vmem_limit_bytes=VMEM_LIMIT
        ),
        name=name,
    )(*operands)


def on_device(
    tokens,
    cotangent,
    qkv_weight,
    out_weight,
    norm_gains,
    router_weight,
    bias_table,
    expert_in,
    expert_out,
    routes,
):
    f32, bf16 = jnp.float32, jnp.bfloat16
    first_section = lax.axis_index("section") == 0
    ne, nd = lax.axis_size("expert"), lax.axis_size("dp")
    groups = ne * nd
    count, width = tokens.shape
    head_count = bias_table.shape[2]
    capacity = max(2, SEQ * 4 // (3 * ne))
    per_device = count // SEQ
    slots = -(-per_device * capacity // 16) * 16
    piece = out_weight.shape[1]
    inner = expert_in.shape[3]

    def filled(rows):
        return jnp.pad(rows, ((0, 0), (0, width - rows.shape[1])))

    def padded(rows):
        return jnp.pad(rows, ((0, -rows.shape[0] % 16), (0, 0)))

    shard = padded(
        jnp.concatenate(
            [
                qkv_weight[0].reshape(3 * piece, width),
                out_weight[0],
                filled(norm_gains[0]),
                filled(router_weight[0].T),
            ]
        )
    )
    full = gather_shards(shard, ne, nd, 0)
    qkv_w = full[:, : 3 * piece].reshape(groups, 3, piece, width)
    qkv_w = qkv_w.transpose(1, 0, 2, 3).reshape(3, width, width)
    out_w = full[:, 3 * piece : 4 * piece].reshape(width, width)
    small = full[:, 4 * piece : 4 * piece + 2 + ne, :piece].transpose(1, 0, 2)
    small = small.reshape(2 + ne, width)
    gain_a, gain_b = small[0].astype(f32), small[1].astype(f32)
    router_t = small[2:]
    w_in, w_out = expert_in[0, 0], expert_out[0, 0]

    bucket_hot = (bucket_grid(SEQ)[..., None] == jnp.arange(BUCKETS, dtype=jnp.int32)).astype(f32)
    bias_heads = jnp.einsum("qkb,bh->hqk", bucket_hot, bias_table[0].astype(f32))
    head_scale = (width // head_count) ** (-0.5)
    route_rows = routes[0, :, 0].reshape(per_device, SEQ)
    route_now = routes[0, :, 0]
    route_hot = (route_now[:, None] == jnp.arange(ne, dtype=jnp.int32)[None, :]).astype(f32)
    place = slot_positions(route_rows, ne)
    place = place + capacity * jnp.arange(per_device, dtype=jnp.int32)[:, None]
    cell = route_now * slots + place.reshape(count)
    sending = (cell[None, :] == jnp.arange(ne * slots, dtype=jnp.int32)[:, None]).astype(bf16)

    def attention_scores(queries, key_heads):
        return (
            jnp.einsum("bhqe,bhke->bhqk", queries, key_heads, preferred_element_type=f32)
            * head_scale
            + bias_heads
        )

    def chosen(section, now, before):
        if before is None:
            return now
        keep = first_section if section == 0 else jnp.logical_not(first_section)
        return tuple(jnp.where(keep, a, b) for a, b in zip(now, before))

    def from_experts(returned):
        rows = jnp.sum(returned.reshape(ne, nd, slots, width).astype(f32), axis=1).astype(bf16)
        return jnp.dot(sending.T, rows.reshape(ne * slots, width), preferred_element_type=f32)

    def forward(section, source, before):
        residual = source.astype(f32)
        normed_a = rms_norm(residual, gain_a).astype(bf16)
        qkv = jnp.einsum("nd,cde->cne", normed_a, qkv_w, preferred_element_type=f32).astype(bf16)
        queries, key_heads, value_heads = (split_heads(qkv[c], head_count) for c in range(3))
        scores = attention_scores(queries, key_heads)
        row_max = jnp.max(scores, axis=-1, keepdims=True)
        expo = jnp.exp(scores - row_max)
        probs_full = expo / jnp.sum(expo, axis=-1, keepdims=True)
        probs = probs_full.astype(bf16)
        mixed = join_heads(
            jnp.einsum("bhqk,bhke->bhqe", probs, value_heads, preferred_element_type=f32)
        ).astype(bf16)
        hidden = residual + jnp.dot(mixed, out_w, preferred_element_type=f32)
        normed_b = rms_norm(hidden, gain_b).astype(bf16)
        logits = lax.dot_general(
            normed_b, router_t, (((1,), (1,)), ((), ())), preferred_element_type=f32
        )
        gate = gate_of(route_hot, logits)
        buffer = jnp.dot(sending, normed_b, preferred_element_type=f32).astype(bf16)
        moe = moe_call(
            moe_forward_kernel,
            (buffer.reshape(ne, slots, width), w_in, w_out),
            ((width, bf16), (inner, f32), (width, bf16)),
            ne, nd, section, 1 + section, "moe_forward",
        )
        moe = chosen(section, tuple(moe), before)
        combined = from_experts(moe[2])
        output = (hidden + gate[:, None] * combined).astype(bf16)
        state = (
            residual, normed_a, queries, key_heads, value_heads, probs_full, mixed, hidden,
            normed_b, logits, combined, gate,
        )
        return output, state, moe

    def backward(section, grad_out, state, moe, before):
        (
            residual, normed_a, queries, key_heads, value_heads, probs_full, mixed, hidden,
            normed_b, logits, combined, gate,
        ) = state
        grad_gate = jnp.sum(grad_out * combined, axis=-1)
        grad_comb = (grad_out * gate[:, None]).astype(bf16)
        grad_rows = jnp.dot(sending, grad_comb, preferred_element_type=f32).astype(bf16)
        back = moe_call(
            moe_backward_kernel,
            (grad_rows.reshape(ne, slots, width), moe[1], w_in, w_out),
            ((width, bf16), (inner, bf16), (inner, bf16), (width, bf16)),
            ne, nd, section, 3 + section, "moe_backward",
        )
        back = chosen(section, tuple(back), before)
        grad_normed = from_experts(back[3])
        gate_out, gate_pull = jax.vjp(partial(gate_of, route_hot), logits)
        grad_logits = gate_pull(grad_gate)[0]
        grad_normed = grad_normed + jnp.dot(grad_logits, router_t.astype(f32))
        norm_out, norm_pull = jax.vjp(rms_norm, hidden, gain_b)
        grad_hidden, grad_gain_b = norm_pull(grad_normed)
        grad_hidden = grad_hidden + grad_out
        grad_attn = grad_hidden.astype(bf16)
        grad_mixed = split_heads(
            lax.dot_general(
                grad_attn, out_w, (((1,), (1,)), ((), ())), preferred_element_type=f32
            ).astype(bf16),
            head_count,
        )
        probs = probs_full.astype(bf16)
        grad_probs = jnp.einsum(
            "bhqe,bhke->bhqk", grad_mixed, value_heads, preferred_element_type=f32
        )
        grad_value = jnp.einsum("bhqk,bhqe->bhke", probs, grad_mixed, preferred_element_type=f32)
        row_delta = jnp.sum(probs_full * grad_probs, axis=-1, keepdims=True)
        grad_score = (probs_full * (grad_probs - row_delta)).astype(bf16)
        grad_query = head_scale * jnp.einsum(
            "bhqk,bhke->bhqe", grad_score, key_heads, preferred_element_type=f32
        )
        grad_key = head_scale * jnp.einsum(
            "bhqk,bhqe->bhke", grad_score, queries, preferred_element_type=f32
        )
        grad_qkv = jnp.stack(
            [join_heads(grad_query), join_heads(grad_key), join_heads(grad_value)]
        ).astype(bf16)
        grad_normed_a = jnp.einsum("cne,cde->nd", grad_qkv, qkv_w, preferred_element_type=f32)
        first_out, first_pull = jax.vjp(rms_norm, residual, gain_a)
        grad_residual, grad_gain_a = first_pull(grad_normed_a)
        grad_source = grad_hidden + grad_residual

        grad_table = jnp.einsum(
            "qkb,hqk->bh", bucket_hot, jnp.sum(grad_score.astype(f32), axis=0)
        )
        qkv_part = jnp.einsum("nd,cne->cde", normed_a, grad_qkv, preferred_element_type=f32)
        out_part = jnp.einsum("nd,ne->de", mixed, grad_attn, preferred_element_type=f32)
        router_part = jnp.einsum("ne,nd->ed", grad_logits, normed_b.astype(f32))
        small_part = jnp.concatenate([jnp.stack([grad_gain_a, grad_gain_b]), router_part])
        small_part = small_part.reshape(2 + ne, groups, piece).transpose(1, 0, 2)
        small_part = jnp.pad(small_part, ((0, 0), (0, 0), (0, width - piece)))
        table_row = jnp.pad(grad_table.reshape(-1), (0, width - BUCKETS * head_count))
        rest = -(4 * piece + 3 + ne) % 16
        parts = jnp.concatenate(
            [
                qkv_part.astype(bf16).reshape(3, groups, piece, width).transpose(1, 0, 2, 3)
                .reshape(groups, 3 * piece, width),
                out_part.astype(bf16).reshape(groups, piece, width),
                small_part.astype(bf16),
                jnp.broadcast_to(table_row.astype(bf16), (groups, 1, width)),
                jnp.zeros((groups, rest, width), bf16),
            ],
            axis=1,
        )
        total = reduce_parts(parts, ne, nd, section, 5 + section)
        return grad_source, total, back

    output_0, state, moe = forward(0, tokens, None)
    received = passed_along(output_0, "section", 1)
    output, state, moe = forward(1, jnp.where(first_section, tokens, received), moe)

    cot_rows = cotangent[0].astype(f32)
    grad_1, total_1, back = backward(1, cot_rows, state, moe, None)
    grad_received = passed_along(grad_1.astype(bf16), "section", -1)
    grad_received, total_1 = lax.optimization_barrier((grad_received, total_1))
    grad_0, total_0, back = backward(
        0, cot_rows + grad_received.astype(f32), state, moe, back
    )
    total = jnp.where(first_section, total_0, total_1)

    def expert_grad(left, right):
        rows = groups * slots
        return lax.dot_general(
            left.reshape(rows, -1), right.reshape(rows, -1), (((0,), (0,)), ((), ())),
            preferred_element_type=f32,
        )[None, None]

    small_at = 4 * piece
    return (
        output[None],
        grad_0[None],
        total[: 3 * piece].reshape(1, 3, piece, width),
        total[3 * piece : small_at][None],
        total[small_at : small_at + 2, :piece][None],
        total[small_at + 2 : small_at + 2 + ne, :piece].T[None],
        total[small_at + 2 + ne, : BUCKETS * head_count].reshape(1, BUCKETS, head_count),
        expert_grad(moe[0], back[1]),
        expert_grad(back[2], back[0]),
    )


def solution(mesh):
    placed = (
        P(("expert", "dp"), None),
        P("section", ("expert", "dp"), None),
        P("section", None, ("expert", "dp"), None),
        P("section", ("expert", "dp"), None),
        P("section", None, ("expert", "dp")),
        P("section", ("expert", "dp"), None),
        P("section", None, None),
        P("section", "expert", None, "dp"),
        P("section", "expert", "dp", None),
        P("section", ("expert", "dp"), None),
    )
    return jax.shard_map(
        on_device,
        mesh=mesh,
        in_specs=placed,
        out_specs=(
            P("section", ("expert", "dp"), None),
            P("section", ("expert", "dp"), None),
            P("section", None, ("expert", "dp"), None),
            P("section", ("expert", "dp"), None),
            P("section", None, ("expert", "dp")),
            P("section", ("expert", "dp"), None),
            P("section", None, None),
            P("section", "expert", None, "dp"),
            P("section", "expert", "dp", None),
        ),
        check_vma=False,
    )
```

```python
from functools import partial

import jax
import jax.numpy as jnp
from jax import lax
from jax.experimental import pallas as pl
from jax.experimental.pallas import tpu as pltpu
from jax.sharding import PartitionSpec as P

BUCKETS = 32
SEQ = 64


EPSILON = 1e-06
BUCKET_EDGES = (12, 16, 23, 32, 46, 64, 91)


def passed_along(value, axis, steps):
    count = lax.axis_size(axis)
    first, last = (max(0, -steps), min(count, count - steps))
    return lax.ppermute(value, axis, [(source, source + steps) for source in range(first, last)])


def bucket_grid(length):
    places = jnp.arange(length, dtype=jnp.int32)
    offset = places[None, :] - places[:, None]
    distance = jnp.abs(offset)
    far_bucket = 8 + sum(((distance >= edge).astype(jnp.int32) for edge in BUCKET_EDGES))
    near_far = jnp.where(distance < 8, distance, far_bucket)
    return near_far + 16 * (offset > 0).astype(jnp.int32)


def slot_positions(route_now, experts):
    route_hot = (route_now[..., None] == jnp.arange(experts, dtype=jnp.int32)).astype(jnp.int32)
    before = jnp.cumsum(route_hot, axis=-2) - route_hot
    return jnp.sum(before * route_hot, axis=-1)


def gelu_tanh(values):
    return jax.nn.gelu(values, approximate=True)


MESH = pl.DeviceIdType.MESH
VMEM_LIMIT = 56 * 1024 * 1024


def at_group(e, d):
    return {"expert": e, "dp": d}


def greet(peers):
    barrier = pltpu.get_barrier_semaphore()
    for peer in peers:
        pl.semaphore_signal(barrier, inc=1, device_id=peer, device_id_type=MESH)
    pl.semaphore_wait(barrier, len(peers))


def remote(src, dst, send_sem, recv_sem, peer):
    return pltpu.make_async_remote_copy(
        src_ref=src, dst_ref=dst, send_sem=send_sem, recv_sem=recv_sem,
        device_id=peer, device_id_type=MESH,
    )


def group_peers(ne, nd):
    e, d = lax.axis_index("expert"), lax.axis_index("dp")
    return [
        (lax.rem(e + ke, ne), lax.rem(d + kd, nd))
        for ke in range(ne) for kd in range(nd) if ke or kd
    ]


def gather_kernel(ne, nd, *refs):
    count = (len(refs) - 3) // 2
    shards, fulls = refs[:count], refs[count : 2 * count]
    send_sem, recv_sem, own_sem = refs[2 * count :]
    e, d = lax.axis_index("expert"), lax.axis_index("dp")
    along_e = [lax.rem(e + k, ne) for k in range(1, ne)]
    along_d = [lax.rem(d + k, nd) for k in range(1, nd)]
    greet([at_group(pe, d) for pe in along_e] + [at_group(e, pd) for pd in along_d])
    me = e * nd + d
    waits = []
    for i in range(count):
        own = pltpu.make_async_copy(shards[i], fulls[i].at[:, me], own_sem.at[i])
        own.start()
        waits.append(own.wait)

    def send(i, slot, source, step, peer):
        copy = remote(
            source, fulls[i].at[:, slot], send_sem.at[i, step], recv_sem.at[i, slot], peer
        )
        copy.start()
        waits.append(copy.wait_send)

    def arrive(i, slot, peer):
        remote(
            fulls[i].at[:, slot], fulls[i].at[:, slot], send_sem.at[i, 0], recv_sem.at[i, slot], peer
        ).wait_recv()

    for i in range(count):
        for k, pe in enumerate(along_e):
            send(i, me, shards[i], k, at_group(pe, d))
    for i in range(count):
        for k, pd in enumerate(along_d):
            send(i, me, shards[i], ne - 1 + k, at_group(e, pd))
    for j, pe in enumerate(along_e):
        slot = pe * nd + d
        for i in range(count):
            arrive(i, slot, at_group(pe, d))
            for k, pd in enumerate(along_d):
                step = ne - 1 + (j + 1) * (nd - 1) + k
                send(i, slot, fulls[i].at[:, slot], step, at_group(e, pd))
    for ke in range(ne):
        for pd in along_d:
            for i in range(count):
                arrive(i, lax.rem(e + ke, ne) * nd + pd, at_group(e, pd))
    for wait in waits:
        wait()


def gather_shards(shards, ne, nd, ident):
    groups = ne * nd
    anywhere = pl.BlockSpec(memory_space=pl.ANY)
    dma = pltpu.SemaphoreType.DMA
    return pl.pallas_call(
        partial(gather_kernel, ne, nd),
        out_shape=[
            jax.ShapeDtypeStruct((s.shape[0], groups) + s.shape[1:], s.dtype) for s in shards
        ],
        in_specs=[anywhere] * len(shards),
        out_specs=[anywhere] * len(shards),
        scratch_shapes=[
            dma((len(shards), ne - 1 + ne * (nd - 1))),
            dma((len(shards), groups)),
            dma((len(shards),)),
        ],
        compiler_params=pltpu.CompilerParams(collective_id=ident, has_side_effects=True),
        name="gather_weights",
    )(*shards)


def exchange(ne, nd, rows_out, arrived, staged, returned, sems, work):
    send_a, recv_a, send_b, recv_b = sems
    e, d = lax.axis_index("expert"), lax.axis_index("dp")
    me = e * nd + d
    peers = group_peers(ne, nd)
    out_a = []
    for i, (pe, pd) in enumerate(peers):
        copy = remote(
            rows_out.at[pe], arrived.at[me], send_a.at[i], recv_a.at[me], at_group(pe, pd)
        )
        copy.start()
        out_a.append(copy)
    arrived[me] = rows_out[e]
    out_b = []
    for ke in range(ne):
        pe = lax.rem(e + ne - ke, ne)
        for kd in range(nd):
            if ke or kd:
                pd = lax.rem(d + nd - kd, nd)
                slot = pe * nd + pd
                remote(
                    rows_out.at[0], arrived.at[slot], send_a.at[0], recv_a.at[slot],
                    at_group(pe, pd),
                ).wait_recv()
        work(pe)
        for kd in range(nd):
            pd = lax.rem(d + nd - kd, nd)
            slot = pe * nd + pd
            if ke or kd:
                copy = remote(
                    staged.at[slot], returned.at[me], send_b.at[len(out_b)], recv_b.at[me],
                    at_group(pe, pd),
                )
                copy.start()
                out_b.append(copy)
            else:
                returned[me] = staged[slot]
    for pe, pd in peers:
        slot = pe * nd + pd
        remote(
            staged.at[slot], returned.at[slot], send_b.at[0], recv_b.at[slot], at_group(pe, pd)
        ).wait_recv()
    for copy in out_a + out_b:
        copy.wait_send()


def across(left, right):
    return lax.dot_general(
        left, right, (((1,), (1,)), ((), ())), preferred_element_type=jnp.float32
    )


def within(left, right):
    return lax.dot_general(
        left, right, (((0,), (0,)), ((), ())), preferred_element_type=jnp.float32
    )


def plain(left, right):
    return jnp.dot(left, right, preferred_element_type=jnp.float32)


def inverse_rms(values):
    return lax.rsqrt(jnp.mean(values * values, axis=-1, keepdims=True) + EPSILON)


def rms_back(grad, values, gain):
    scale = inverse_rms(values)
    turned = grad * gain
    inner = jnp.mean(turned * values, axis=-1, keepdims=True)
    back = scale * turned - values * (scale * scale * scale * inner)
    return back, jnp.sum(grad * values * scale, axis=0, keepdims=True)


def head_masks(count, size):
    lane = lax.broadcasted_iota(jnp.int32, (count, 128), 1)
    return [(lane >= i * size) & (lane < (i + 1) * size) for i in range(128 // size)]


def only(mask, values):
    return jnp.where(mask, values, jnp.zeros_like(values))


def forward_kernel(
    ne, nd, size,
    tokens, qkv_w, out_w, gains, router, bias, sending, sending_t, route_hot, w_in, w_out,
    x, normed_a, qkv, probs, mixed, hidden, normed_b, shares, gate, combined, arrived, pre, y,
    rows_out, staged, returned, hand_sems, *sems,
):
    f32, bf16 = jnp.float32, jnp.bfloat16
    section = lax.axis_index("section")
    partner = {"section": 1 - section}
    greet([at_group(*peer) for peer in group_peers(ne, nd)] + [partner])
    count, width = x.shape
    slots = rows_out.shape[1]
    handed = remote(y, x, hand_sems.at[0], hand_sems.at[1], partner)

    @pl.when(section == 0)
    def _():
        x[...] = tokens[...]

    @pl.when(section == 1)
    def _():
        handed.wait_recv()

    source = x[...].astype(f32)
    a = (source * inverse_rms(source) * gains[0:1, :]).astype(bf16)
    normed_a[...] = a
    for c in range(3):
        qkv[c] = plain(a, qkv_w[c]).astype(bf16)
    masks = head_masks(count, size)
    for pair in range(width // 128):
        lanes = pl.ds(pair * 128, 128)
        q, k, v = qkv[0, :, lanes], qkv[1, :, lanes], qkv[2, :, lanes]
        joined = jnp.zeros((count, 128), f32)
        for i, mask in enumerate(masks):
            head = pair * len(masks) + i
            score = across(only(mask, q), k) * (size**-0.5) + bias[head]
            expo = jnp.exp(score - jnp.max(score, axis=-1, keepdims=True))
            p = expo / jnp.sum(expo, axis=-1, keepdims=True)
            probs[head] = p
            joined = jnp.where(mask, plain(p.astype(bf16), v), joined)
        mixed[:, lanes] = joined.astype(bf16)
    h = source + plain(mixed[...], out_w[...])
    hidden[...] = h
    b = (h * inverse_rms(h) * gains[1:2, :]).astype(bf16)
    normed_b[...] = b
    rows_out[...] = plain(sending[...], b).astype(bf16).reshape(ne, slots, width)

    def work(pe):
        block = pl.ds(pe * nd, nd)
        rows = arrived[block].reshape(nd * slots, width)
        inner = plain(rows, w_in[...])
        pre[block] = inner.reshape(nd, slots, -1)
        act = gelu_tanh(inner).astype(bf16)
        staged[block] = plain(act, w_out[...]).astype(bf16).reshape(nd, slots, width)

    exchange(ne, nd, rows_out, arrived, staged, returned, sems, work)
    logits = across(b, router[...])
    lane = lax.broadcasted_iota(jnp.int32, logits.shape, 1)
    logits = jnp.where(lane < ne, logits, -1e30)
    expo = jnp.exp(logits - jnp.max(logits, axis=-1, keepdims=True))
    share = expo / jnp.sum(expo, axis=-1, keepdims=True)
    shares[...] = share
    weight = jnp.sum(share * route_hot[...], axis=-1, keepdims=True)
    gate[...] = weight
    result = from_experts(ne, nd, returned, sending_t)
    combined[...] = result
    y[...] = (h + weight * result).astype(bf16)

    @pl.when(section == 0)
    def _():
        handed.start()
        handed.wait_send()


def from_experts(ne, nd, returned, sending_t):
    slots, width = returned.shape[1:]
    rows = []
    for e in range(ne):
        total = returned[e * nd].astype(jnp.float32)
        for d in range(1, nd):
            total = total + returned[e * nd + d].astype(jnp.float32)
        rows.append(total.astype(jnp.bfloat16))
    return plain(sending_t[...], jnp.concatenate(rows, axis=0))


def offset_sums(score_grad):
    count = score_grad.shape[0]
    row = lax.broadcasted_iota(jnp.int32, score_grad.shape, 0)
    step = 1
    while step < count:
        moved = pltpu.roll(score_grad, count - step, 1)
        score_grad = jnp.where(lax.rem(row // step, 2) == 1, moved, score_grad)
        step *= 2
    return jnp.sum(score_grad, axis=0, keepdims=True)


def backward_kernel(
    ne, nd, size, summed,
    cot, qkv_w, out_w, gains, router, sending, sending_t, route_hot, w_in, w_out,
    x, normed_a, qkv, probs, mixed, hidden, normed_b, shares, gate, combined, forward_rows, pre,
    grad_source, parts_total, small_total, in_grad, out_grad,
    incoming, handing, grad_qkv, small, rows_out, arrived, inner_grad, act, staged, returned,
    hand_sems, send_a, recv_a, send_b, recv_b, *sum_refs,
):
    f32, bf16 = jnp.float32, jnp.bfloat16
    section = lax.axis_index("section")
    e, d = lax.axis_index("expert"), lax.axis_index("dp")
    partner = {"section": 1 - section}
    greet([at_group(*peer) for peer in group_peers(ne, nd)] + [partner])
    count, width = x.shape
    slots = rows_out.shape[1]
    handed = remote(handing, incoming, hand_sems.at[0], hand_sems.at[1], partner)

    @pl.when(section == 1)
    def _():
        incoming[...] = jnp.zeros_like(incoming)

    @pl.when(section == 0)
    def _():
        handed.wait_recv()

    grad_out = cot[...].astype(f32) + incoming[...].astype(f32)
    grad_gate = jnp.sum(grad_out * combined[...], axis=-1, keepdims=True)
    grad_comb = (grad_out * gate[...]).astype(bf16)
    rows_out[...] = plain(sending[...], grad_comb).astype(bf16).reshape(ne, slots, width)

    def work(pe):
        block = pl.ds(pe * nd, nd)
        rows = arrived[block].reshape(nd * slots, width)
        grad_act = across(rows, w_out[...])
        u = pre[block].reshape(nd * slots, -1)
        square = u * u
        bend = jnp.tanh(0.7978845608028654 * (u + 0.044715 * square * u))
        act[block] = (0.5 * u * (1.0 + bend)).astype(bf16).reshape(nd, slots, -1)
        slope = 0.5 * (1.0 + bend) + 0.5 * u * (1.0 - bend * bend) * (
            0.7978845608028654 * (1.0 + 3 * 0.044715 * square)
        )
        grad = (grad_act * slope).astype(bf16)
        inner_grad[block] = grad.reshape(nd, slots, -1)
        staged[block] = across(grad, w_in[...]).astype(bf16).reshape(nd, slots, width)

    exchange(ne, nd, rows_out, arrived, staged, returned, (send_a, recv_a, send_b, recv_b), work)
    share = shares[...]
    grad_logits = (grad_gate * share * (route_hot[...] - gate[...])).astype(bf16)
    grad_normed = from_experts(ne, nd, returned, sending_t) + plain(grad_logits, router[...])
    back, grad_gain_b = rms_back(grad_normed, hidden[...], gains[1:2, :])
    grad_hidden = back + grad_out
    grad_attn = grad_hidden.astype(bf16)
    grad_mixed = across(grad_attn, out_w[...]).astype(bf16)

    parts = sum_refs[0] if summed else parts_total
    stage = Sums(ne, nd, sum_refs) if summed else None

    def part(c, left, right):
        value = within(left, right).astype(bf16)
        if summed:
            parts[c] = value.reshape((ne, nd) + parts.shape[3:])
            stage.send_first(c)
        else:
            parts[c] = value

    part(3, mixed[...], grad_attn)
    masks = head_masks(count, size)
    offsets = []
    for pair in range(width // 128):
        lanes = slice(pair * 128, (pair + 1) * 128)
        q, k, v = qkv[0, :, lanes], qkv[1, :, lanes], qkv[2, :, lanes]
        grad_o = grad_mixed[:, lanes]
        grad_q = grad_k = grad_v = jnp.zeros((count, 128), f32)
        for i, mask in enumerate(masks):
            head = pair * len(masks) + i
            p = probs[head]
            own = only(mask, grad_o)
            grad_p = across(own, v)
            delta = jnp.sum(p * grad_p, axis=-1, keepdims=True)
            grad_s = (p * (grad_p - delta)).astype(bf16)
            grad_v = grad_v + within(p.astype(bf16), own)
            grad_q = grad_q + plain(grad_s, only(mask, k))
            grad_k = grad_k + within(grad_s, only(mask, q))
            offsets.append(offset_sums(grad_s.astype(f32)))
        grad_qkv[0, :, lanes] = (grad_q * (size**-0.5)).astype(bf16)
        grad_qkv[1, :, lanes] = (grad_k * (size**-0.5)).astype(bf16)
        grad_qkv[2, :, lanes] = grad_v.astype(bf16)
    grad_a = across(grad_qkv[0], qkv_w[0])
    for c in range(1, 3):
        grad_a = grad_a + across(grad_qkv[c], qkv_w[c])
    back, grad_gain_a = rms_back(grad_a, x[...].astype(f32), gains[0:1, :])
    grad_x = grad_hidden + back
    grad_source[...] = grad_x

    @pl.when(section == 1)
    def _():
        handing[...] = grad_x.astype(bf16)
        handed.start()

    for c in range(3):
        part(c, normed_a[...], grad_qkv[c])
    small[...] = jnp.zeros_like(small)
    small[0:1, :] = grad_gain_a
    small[1:2, :] = grad_gain_b
    small[8 : 8 + ne, :] = within(grad_logits, normed_b[...])[:ne]
    for head, value in enumerate(offsets):
        small[16 + head : 17 + head, :count] = value
    if summed:
        stage.small.send_first(small)
    rows = arrived.shape[0] * slots
    in_grad[...] = within(
        forward_rows[...].reshape(rows, width), inner_grad[...].reshape(rows, -1)
    )
    out_grad[...] = within(act[...].reshape(rows, -1), arrived[...].reshape(rows, width))
    if summed:
        for c in (3, 0, 1, 2):
            stage.send_second(c)
        stage.small.send_second()
        for c in (3, 0, 1, 2):
            parts_total[c] = stage.finish(c)
        small_total[...] = stage.small.finish()
        stage.wait_sent()
        stage.small.wait_sent()
    else:
        small_total[...] = small[...]

    @pl.when(section == 1)
    def _():
        handed.wait_send()


def in_order(ref, count, pick):
    total = pick(ref, 0).astype(jnp.float32)
    for j in range(1, count):
        total = total + pick(ref, j).astype(jnp.float32)
    return total


class Sums:
    def __init__(self, ne, nd, refs):
        self.ne, self.nd = ne, nd
        self.e, self.d = lax.axis_index("expert"), lax.axis_index("dp")
        (
            self.parts, self.first, self.staged, self.second,
            self.send_a, self.recv_a, self.send_b, self.recv_b,
        ) = refs[:8]
        self.along_e = [lax.rem(self.e + k, ne) for k in range(1, ne)]
        self.along_d = [lax.rem(self.d + k, nd) for k in range(1, nd)]
        self.sent = []
        self.small = SmallSums(self, refs[8:])

    def send_first(self, c):
        for k, pd in enumerate(self.along_d):
            copy = remote(
                self.parts.at[c, :, pd], self.first.at[c, self.d],
                self.send_a.at[c, k], self.recv_a.at[c, self.d], at_group(self.e, pd),
            )
            copy.start()
            self.sent.append(copy)
        self.first[c, self.d] = self.parts[c, :, self.d]

    def send_second(self, c):
        for pd in self.along_d:
            remote(
                self.parts.at[c, :, pd], self.first.at[c, pd],
                self.send_a.at[c, 0], self.recv_a.at[c, pd], at_group(self.e, pd),
            ).wait_recv()
        total = in_order(self.first, self.nd, lambda ref, j: ref[c, j])
        self.staged[c] = total.astype(jnp.bfloat16)
        for k, pe in enumerate(self.along_e):
            copy = remote(
                self.staged.at[c, pe], self.second.at[c, self.e],
                self.send_b.at[c, k], self.recv_b.at[c, self.e], at_group(pe, self.d),
            )
            copy.start()
            self.sent.append(copy)
        self.second[c, self.e] = self.staged[c, self.e]

    def finish(self, c):
        for pe in self.along_e:
            remote(
                self.staged.at[c, pe], self.second.at[c, pe],
                self.send_b.at[c, 0], self.recv_b.at[c, pe], at_group(pe, self.d),
            ).wait_recv()
        return in_order(self.second, self.ne, lambda ref, j: ref[c, j])

    def wait_sent(self):
        for copy in self.sent:
            copy.wait_send()


class SmallSums:
    def __init__(self, outer, refs):
        self.outer = outer
        (
            self.mine, self.first, self.staged, self.second,
            self.send_a, self.recv_a, self.send_b, self.recv_b,
        ) = refs
        self.sent = []

    def spread(self, source, target, send, recv, peers, me):
        for k, peer in enumerate(peers):
            copy = remote(source, target.at[me], send.at[k], recv.at[me], peer)
            copy.start()
            self.sent.append(copy)
        target[me] = source[...]

    def arrive(self, source, target, send, recv, count, peers, slots):
        for peer, slot in zip(peers, slots):
            remote(source, target.at[slot], send.at[0], recv.at[slot], peer).wait_recv()
        return in_order(target, count, lambda ref, j: ref[j])

    def send_first(self, values):
        o = self.outer
        self.mine[...] = values[...].astype(jnp.bfloat16)
        self.peers_d = [at_group(o.e, pd) for pd in o.along_d]
        self.peers_e = [at_group(pe, o.d) for pe in o.along_e]
        self.spread(self.mine, self.first, self.send_a, self.recv_a, self.peers_d, o.d)

    def send_second(self):
        o = self.outer
        total = self.arrive(
            self.mine, self.first, self.send_a, self.recv_a, o.nd, self.peers_d, o.along_d
        )
        self.staged[...] = total.astype(jnp.bfloat16)
        self.spread(self.staged, self.second, self.send_b, self.recv_b, self.peers_e, o.e)

    def finish(self):
        o = self.outer
        return self.arrive(
            self.staged, self.second, self.send_b, self.recv_b, o.ne, self.peers_e, o.along_e
        )

    def wait_sent(self):
        for copy in self.sent:
            copy.wait_send()


def call(kernel, operands, outs, scratch, ident, name):
    vmem = pl.BlockSpec(memory_space=pltpu.VMEM)
    return pl.pallas_call(
        kernel,
        out_shape=[jax.ShapeDtypeStruct(shape, dtype) for shape, dtype in outs],
        in_specs=[vmem] * len(operands),
        out_specs=[vmem] * len(outs),
        scratch_shapes=scratch,
        compiler_params=pltpu.CompilerParams(
            collective_id=ident, has_side_effects=True, vmem_limit_bytes=VMEM_LIMIT
        ),
        name=name,
    )(*operands)


def on_device(
    tokens,
    cotangent,
    qkv_weight,
    out_weight,
    norm_gains,
    router_weight,
    bias_table,
    expert_in,
    expert_out,
    routes,
):
    f32, bf16 = jnp.float32, jnp.bfloat16
    ne, nd = lax.axis_size("expert"), lax.axis_size("dp")
    groups = ne * nd
    count, width = tokens.shape
    heads = bias_table.shape[2]
    size = width // heads
    capacity = max(2, SEQ * 4 // (3 * ne))
    per_device = count // SEQ
    slots = -(-per_device * capacity // 16) * 16
    piece = out_weight.shape[1]
    inner = expert_in.shape[3]
    lanes = 128
    dma = pltpu.SemaphoreType.DMA

    small_shard = jnp.concatenate([norm_gains[0], router_weight[0].T])
    small_shard = jnp.pad(
        small_shard, ((0, -small_shard.shape[0] % 16), (0, -piece % lanes))
    )
    qkv_w, out_w, small = gather_shards(
        (qkv_weight[0], out_weight, small_shard[None]), ne, nd, 0
    )
    qkv_w = qkv_w.reshape(3, width, width)
    out_w = out_w.reshape(width, width)
    small = small[0, :, : 2 + ne, :piece].transpose(1, 0, 2).reshape(2 + ne, width)
    gains = small[:2].astype(f32)
    router = jnp.pad(small[2:], ((0, lanes - ne), (0, 0)))
    w_in, w_out = expert_in[0, 0], expert_out[0, 0]

    bucket_hot = (bucket_grid(SEQ)[..., None] == jnp.arange(BUCKETS, dtype=jnp.int32)).astype(f32)
    bias_heads = jnp.einsum("qkb,bh->hqk", bucket_hot, bias_table[0].astype(f32))
    place_now = jnp.arange(count, dtype=jnp.int32) // SEQ
    bias = jnp.where(
        place_now[:, None] == place_now[None, :],
        jnp.tile(bias_heads, (1, per_device, per_device)),
        -1e30,
    )
    route_now = routes[0, :, 0]
    route_hot = (
        route_now[:, None] == jnp.arange(lanes, dtype=jnp.int32)[None, :]
    ).astype(f32)
    place = slot_positions(route_now.reshape(per_device, SEQ), ne)
    place = place + capacity * jnp.arange(per_device, dtype=jnp.int32)[:, None]
    cell = route_now * slots + place.reshape(count)
    cells = jnp.arange(ne * slots, dtype=jnp.int32)
    sending = (cell[None, :] == cells[:, None]).astype(bf16)
    sending_t = (cell[:, None] == cells[None, :]).astype(bf16)

    row, wide = (count, width), (groups, slots, width)
    deep = (groups, slots, inner)
    moe_sems = [dma((groups - 1,)), dma((groups,)), dma((groups - 1,)), dma((groups,))]
    kept = call(
        partial(forward_kernel, ne, nd, size),
        (tokens, qkv_w, out_w, gains, router, bias, sending, sending_t, route_hot, w_in, w_out),
        (
            (row, bf16), (row, bf16), ((3,) + row, bf16), ((heads, count, count), f32),
            (row, bf16), (row, f32), (row, bf16), ((count, lanes), f32), ((count, 1), f32),
            (row, f32), (wide, bf16), (deep, f32), (row, bf16),
        ),
        [
            pltpu.VMEM((ne, slots, width), bf16), pltpu.VMEM(wide, bf16), pltpu.VMEM(wide, bf16),
            dma((2,)),
        ] + moe_sems,
        1, "forward_layers",
    )
    kept, output = kept[:-1], kept[-1]

    summed = piece % 16 == 0
    small_rows = 16 + -(-heads // 16) * 16
    scratch = [
        pltpu.VMEM(row, bf16), pltpu.VMEM(row, bf16), pltpu.VMEM((3,) + row, bf16),
        pltpu.VMEM((small_rows, width), f32),
        pltpu.VMEM((ne, slots, width), bf16), pltpu.VMEM(wide, bf16), pltpu.VMEM(deep, bf16),
        pltpu.VMEM(deep, bf16), pltpu.VMEM(wide, bf16), pltpu.VMEM(wide, bf16), dma((2,)),
    ] + moe_sems
    if summed:
        tile = (piece, width)
        scratch += [
            pltpu.VMEM((4, ne, nd) + tile, bf16), pltpu.VMEM((4, nd, ne) + tile, bf16),
            pltpu.VMEM((4, ne) + tile, bf16), pltpu.VMEM((4, ne) + tile, bf16),
            dma((4, nd - 1)), dma((4, nd)), dma((4, ne - 1)), dma((4, ne)),
        ]
        tile = (small_rows, width)
        scratch += [
            pltpu.VMEM(tile, bf16), pltpu.VMEM((nd,) + tile, bf16), pltpu.VMEM(tile, bf16),
            pltpu.VMEM((ne,) + tile, bf16),
            dma((nd - 1,)), dma((nd,)), dma((ne - 1,)), dma((ne,)),
        ]
    grad_source, total, small_total, in_grad, out_grad = call(
        partial(backward_kernel, ne, nd, size, summed),
        (
            cotangent[0], qkv_w, out_w, gains, router, sending, sending_t, route_hot, w_in, w_out,
            *kept,
        ),
        (
            (row, f32),
            ((4, piece, width), f32) if summed else ((4, width, width), bf16),
            ((small_rows, width), f32), ((width, inner), f32), ((inner, width), f32),
        ),
        scratch, 2, "backward_layers",
    )
    both = ("expert", "dp")
    if not summed:
        total = lax.psum_scatter(total.astype(f32), both, scatter_dimension=1, tiled=True)
        small_total = lax.psum(small_total, both)
    at = (lax.axis_index("expert") * nd + lax.axis_index("dp")) * piece
    mine = lax.dynamic_slice_in_dim(small_total[:16], at, piece, 1)
    offset = jnp.arange(count, dtype=jnp.int32)
    offset = jnp.where(offset < SEQ, offset, offset - count)
    near = jnp.abs(offset)
    far = 8 + sum(((near >= edge).astype(jnp.int32) for edge in BUCKET_EDGES))
    bucket = jnp.where(near < 8, near, far) + 16 * (offset > 0).astype(jnp.int32)
    offset_hot = (bucket[:, None] == jnp.arange(BUCKETS, dtype=jnp.int32)).astype(f32)
    offset_sum = small_total[16 : 16 + heads, :count]
    table_grad = jnp.sum(offset_hot[:, :, None] * offset_sum.T[:, None, :], axis=0)
    return (
        output[None],
        grad_source[None],
        total[:3][None],
        total[3][None],
        mine[:2][None],
        mine[8 : 8 + ne].T[None],
        table_grad[None],
        in_grad[None, None],
        out_grad[None, None],
    )


def solution(mesh):
    placed = (
        P(("expert", "dp"), None),
        P("section", ("expert", "dp"), None),
        P("section", None, ("expert", "dp"), None),
        P("section", ("expert", "dp"), None),
        P("section", None, ("expert", "dp")),
        P("section", ("expert", "dp"), None),
        P("section", None, None),
        P("section", "expert", None, "dp"),
        P("section", "expert", "dp", None),
        P("section", ("expert", "dp"), None),
    )
    return jax.shard_map(
        on_device,
        mesh=mesh,
        in_specs=placed,
        out_specs=(
            P("section", ("expert", "dp"), None),
            P("section", ("expert", "dp"), None),
            P("section", None, ("expert", "dp"), None),
            P("section", ("expert", "dp"), None),
            P("section", None, ("expert", "dp")),
            P("section", ("expert", "dp"), None),
            P("section", None, None),
            P("section", "expert", None, "dp"),
            P("section", "expert", "dp", None),
        ),
        check_vma=False,
    )
```

```python
from functools import partial

import jax
import jax.numpy as jnp
from jax import lax
from jax.experimental import pallas as pl
from jax.experimental.pallas import tpu as pltpu
from jax.sharding import PartitionSpec as P

BUCKETS = 32
SEQ = 64


EPSILON = 1e-06
BUCKET_EDGES = (12, 16, 23, 32, 46, 64, 91)


def gelu_tanh(values):
    return jax.nn.gelu(values, approximate=True)


MESH = pl.DeviceIdType.MESH
VMEM_LIMIT = 62 * 1024 * 1024


def at_group(e, d):
    return {"expert": e, "dp": d}


def greet(peers):
    barrier = pltpu.get_barrier_semaphore()
    for peer in peers:
        pl.semaphore_signal(barrier, inc=1, device_id=peer, device_id_type=MESH)
    pl.semaphore_wait(barrier, len(peers))


def remote(src, dst, send_sem, recv_sem, peer):
    return pltpu.make_async_remote_copy(
        src_ref=src, dst_ref=dst, send_sem=send_sem, recv_sem=recv_sem,
        device_id=peer, device_id_type=MESH,
    )


def near_peers(ne, nd):
    e, d = lax.axis_index("expert"), lax.axis_index("dp")
    return [at_group(lax.rem(e + k, ne), d) for k in range(1, ne)] + [
        at_group(e, lax.rem(d + k, nd)) for k in range(1, nd)
    ]


def bucket_of(offset):
    distance = jnp.abs(offset)
    far_bucket = 8 + sum(((distance >= edge).astype(jnp.int32) for edge in BUCKET_EDGES))
    near_far = jnp.where(distance < 8, distance, far_bucket)
    return near_far + 16 * (offset > 0).astype(jnp.int32)


def prepare(ne, capacity, table, route, bias, sending_t, route_hot):
    heads, count = bias.shape[:2]
    square = (count, count)
    query = lax.broadcasted_iota(jnp.int32, square, 0)
    key = lax.broadcasted_iota(jnp.int32, square, 1)
    together = query // SEQ == key // SEQ
    bucket = bucket_of(key - query)
    for head in range(heads):
        value = jnp.full(square, -1e30, jnp.float32)
        for b in range(BUCKETS):
            value = jnp.where(bucket == b, table[b, head], value)
        bias[head] = jnp.where(together, value, -1e30)
    now = route[...]
    hot = now == lax.broadcasted_iota(jnp.int32, route_hot.shape, 1)
    route_hot[...] = hot.astype(jnp.float32)
    earlier = (together & (key < query)).astype(jnp.bfloat16)
    before = jnp.dot(earlier, hot.astype(jnp.bfloat16), preferred_element_type=jnp.float32)
    place = jnp.sum(jnp.where(hot, before, 0.0), axis=-1, keepdims=True).astype(jnp.int32)
    place = place + capacity * (lax.broadcasted_iota(jnp.int32, now.shape, 0) // SEQ)
    cell = now * (sending_t.shape[1] // ne) + place
    sending_t[...] = (
        cell == lax.broadcasted_iota(jnp.int32, sending_t.shape, 1)
    ).astype(jnp.float32).astype(jnp.bfloat16)


def gather_kernel(
    ne, nd, capacity,
    qkv_shard, out_shard, small_shard, table, route,
    qkv_full, out_full, gains, router, bias, sending_t, route_hot,
    small_full, send_sem, recv_sem, own_sem, turn_sem,
):
    count = 3
    shards, fulls = (qkv_shard, out_shard, small_shard), (qkv_full, out_full, small_full)
    section = lax.axis_index("section")
    partner = {"section": 1 - section}
    e, d = lax.axis_index("expert"), lax.axis_index("dp")
    along_e = [lax.rem(e + k, ne) for k in range(1, ne)]
    along_d = [lax.rem(d + k, nd) for k in range(1, nd)]
    greet(near_peers(ne, nd) + [partner])

    @pl.when(section == 1)
    def _():
        prepare(ne, capacity, table, route, bias, sending_t, route_hot)
        pl.semaphore_wait(turn_sem, 1)

    me = e * nd + d
    waits = []
    for i in range(count):
        own = pltpu.make_async_copy(shards[i], fulls[i].at[:, me], own_sem.at[i])
        own.start()
        waits.append(own.wait)

    def send(i, slot, source, step, peer):
        copy = remote(
            source, fulls[i].at[:, slot], send_sem.at[i, step], recv_sem.at[i, slot], peer
        )
        copy.start()
        waits.append(copy.wait_send)

    def arrive(i, slot, peer):
        remote(
            fulls[i].at[:, slot], fulls[i].at[:, slot], send_sem.at[i, 0], recv_sem.at[i, slot], peer
        ).wait_recv()

    for i in range(count):
        for k, pe in enumerate(along_e):
            send(i, me, shards[i], k, at_group(pe, d))
    for i in range(count):
        for k, pd in enumerate(along_d):
            send(i, me, shards[i], ne - 1 + k, at_group(e, pd))
    @pl.when(section == 0)
    def _():
        prepare(ne, capacity, table, route, bias, sending_t, route_hot)

    for j, pe in enumerate(along_e):
        slot = pe * nd + d
        for i in range(count):
            arrive(i, slot, at_group(pe, d))
            for k, pd in enumerate(along_d):
                step = ne - 1 + (j + 1) * (nd - 1) + k
                send(i, slot, fulls[i].at[:, slot], step, at_group(e, pd))
    for ke in range(ne):
        for pd in along_d:
            for i in range(count):
                arrive(i, lax.rem(e + ke, ne) * nd + pd, at_group(e, pd))

    @pl.when(section == 0)
    def _():
        pl.semaphore_signal(turn_sem, inc=1, device_id=partner, device_id_type=MESH)

    for wait in waits:
        wait()
    small = in_order(small_full, ne * nd, lambda ref, g: ref[0, g])
    gains[...] = small[8:10]
    router[...] = jnp.zeros_like(router)
    router[0:16, :] = jnp.where(
        lax.broadcasted_iota(jnp.int32, small.shape, 0) < ne, small, 0.0
    ).astype(router.dtype)


def gather_shards(qkv, out, small, table, route, ne, nd, capacity, slots, ident):
    groups = ne * nd
    count, width, heads, lanes = route.shape[0], small.shape[2], table.shape[1], 128
    anywhere = pl.BlockSpec(memory_space=pl.ANY)
    vmem = pl.BlockSpec(memory_space=pltpu.VMEM)
    dma = pltpu.SemaphoreType.DMA
    f32, bf16 = jnp.float32, jnp.bfloat16
    outs = (
        ((3, groups) + qkv.shape[1:], bf16), ((1, groups) + out.shape[1:], bf16),
        ((2, width), f32), ((lanes, width), bf16), ((heads, count, count), f32),
        ((count, ne * slots), bf16), ((count, lanes), f32),
    )
    return pl.pallas_call(
        partial(gather_kernel, ne, nd, capacity),
        out_shape=[jax.ShapeDtypeStruct(shape, dtype) for shape, dtype in outs],
        in_specs=[anywhere, anywhere, vmem, pl.BlockSpec(memory_space=pltpu.SMEM), vmem],
        out_specs=[anywhere] * 2 + [vmem] * 5,
        scratch_shapes=[
            pltpu.VMEM((1, groups) + small.shape[1:], bf16),
            dma((3, ne - 1 + ne * (nd - 1))), dma((3, groups)), dma((3,)),
            pltpu.SemaphoreType.REGULAR,
        ],
        compiler_params=pltpu.CompilerParams(
            collective_id=ident, has_side_effects=True, vmem_limit_bytes=VMEM_LIMIT
        ),
        name="gather_weights",
    )(qkv, out, small, table, route)


def exchange(ne, nd, rows_out, arrived, staged, halves, summed, returned, sems, work):
    send_e, send_d, recv_a, send_p, recv_p, send_b, recv_b = sems
    e, d = lax.axis_index("expert"), lax.axis_index("dp")
    me = e * nd + d
    order = [lax.rem(e + ne - k, ne) for k in range(ne)]
    along_d = [lax.rem(d + k, nd) for k in range(1, nd)]
    waits = []

    def start(copy):
        copy.start()
        waits.append(copy.wait_send)

    for k in range(1, ne):
        pe = lax.rem(e + k, ne)
        start(remote(
            rows_out.at[pe], arrived.at[me], send_e.at[k - 1], recv_a.at[me], at_group(pe, d)
        ))
    for j, pd in enumerate(along_d):
        start(remote(
            rows_out.at[e], arrived.at[me], send_d.at[0, j], recv_a.at[me], at_group(e, pd)
        ))
    arrived[me] = rows_out[e]

    def forward(k):
        slot = order[k] * nd + d
        remote(
            arrived.at[slot], arrived.at[slot], send_e.at[0], recv_a.at[slot],
            at_group(order[k], d),
        ).wait_recv()
        for j, pd in enumerate(along_d):
            start(remote(
                arrived.at[slot], arrived.at[slot], send_d.at[k, j], recv_a.at[slot],
                at_group(e, pd),
            ))

    def step(k):
        pe = order[k]
        for pd in along_d:
            slot = pe * nd + pd
            remote(
                arrived.at[slot], arrived.at[slot], send_d.at[k, 0], recv_a.at[slot],
                at_group(e, pd),
            ).wait_recv()
        work(pe)
        for j, pd in enumerate(along_d):
            start(remote(
                staged.at[pe * nd + pd], halves.at[pe * nd + d], send_p.at[k, j],
                recv_p.at[pe * nd + d], at_group(e, pd),
            ))
        halves[pe * nd + d] = staged[pe * nd + d]

    def finish(k):
        pe = order[k]
        for pd in along_d:
            slot = pe * nd + pd
            remote(
                staged.at[slot], halves.at[slot], send_p.at[k, 0], recv_p.at[slot],
                at_group(e, pd),
            ).wait_recv()
        total = in_order(halves, nd, lambda ref, j: ref[pe * nd + j]).astype(jnp.bfloat16)
        if k:
            summed[k - 1] = total
            start(remote(
                summed.at[k - 1], returned.at[e], send_b.at[k - 1], recv_b.at[e], at_group(pe, d)
            ))
        else:
            returned[e] = total

    for k in range(1, ne):
        forward(k)
        if k == 1:
            step(0)
    for k in range(1, ne):
        step(k)
        if k > 1:
            finish(k - 1)
    finish(ne - 1)
    finish(0)
    for pe in order[1:]:
        remote(
            summed.at[0], returned.at[pe], send_b.at[0], recv_b.at[pe], at_group(pe, d)
        ).wait_recv()
    for wait in waits:
        wait()


def across(left, right):
    return lax.dot_general(
        left, right, (((1,), (1,)), ((), ())), preferred_element_type=jnp.float32
    )


def within(left, right):
    return lax.dot_general(
        left, right, (((0,), (0,)), ((), ())), preferred_element_type=jnp.float32
    )


def plain(left, right):
    return jnp.dot(left, right, preferred_element_type=jnp.float32)


def inverse_rms(values):
    return lax.rsqrt(jnp.mean(values * values, axis=-1, keepdims=True) + EPSILON)


def rms_back(grad, values, gain):
    scale = inverse_rms(values)
    turned = grad * gain
    inner = jnp.mean(turned * values, axis=-1, keepdims=True)
    back = scale * turned - values * (scale * scale * scale * inner)
    return back, jnp.sum(grad * values * scale, axis=0, keepdims=True)


def head_masks(count, size):
    lane = lax.broadcasted_iota(jnp.int32, (count, 128), 1)
    return [(lane >= i * size) & (lane < (i + 1) * size) for i in range(128 // size)]


def only(mask, values):
    return jnp.where(mask, values, jnp.zeros_like(values))


def forward_kernel(
    ne, nd, size,
    tokens, qkv_w, out_w, gains, router, bias, sending_t, route_hot, w_in, w_out,
    x, normed_a, qkv, probs, mixed, hidden, normed_b, shares, gate, combined, arrived, pre, y,
    rows_out, staged, halves, own_sums, returned, hand_sems, *sems,
):
    f32, bf16 = jnp.float32, jnp.bfloat16
    section = lax.axis_index("section")
    partner = {"section": 1 - section}
    greet(near_peers(ne, nd) + [partner])
    count, width = x.shape
    slots = rows_out.shape[1]
    handed = remote(y, x, hand_sems.at[0], hand_sems.at[1], partner)

    @pl.when(section == 0)
    def _():
        x[...] = tokens[...]

    @pl.when(section == 1)
    def _():
        handed.wait_recv()

    source = x[...].astype(f32)
    a = (source * inverse_rms(source) * gains[0:1, :]).astype(bf16)
    normed_a[...] = a
    for c in range(3):
        qkv[c] = plain(a, qkv_w[c]).astype(bf16)
    masks = head_masks(count, size)
    for pair in range(width // 128):
        lanes = pl.ds(pair * 128, 128)
        q, k, v = qkv[0, :, lanes], qkv[1, :, lanes], qkv[2, :, lanes]
        joined = jnp.zeros((count, 128), f32)
        for i, mask in enumerate(masks):
            head = pair * len(masks) + i
            score = across(only(mask, q), k) * (size**-0.5) + bias[head]
            expo = jnp.exp(score - jnp.max(score, axis=-1, keepdims=True))
            p = expo / jnp.sum(expo, axis=-1, keepdims=True)
            probs[head] = p
            joined = jnp.where(mask, plain(p.astype(bf16), v), joined)
        mixed[:, lanes] = joined.astype(bf16)
    h = source + plain(mixed[...], out_w[...])
    hidden[...] = h
    b = (h * inverse_rms(h) * gains[1:2, :]).astype(bf16)
    normed_b[...] = b
    rows_out[...] = within(sending_t[...], b).astype(bf16).reshape(ne, slots, width)

    def work(pe):
        block = pl.ds(pe * nd, nd)
        rows = arrived[block].reshape(nd * slots, width)
        inner = plain(rows, w_in[...])
        pre[block] = inner.reshape(nd, slots, -1)
        act = gelu_tanh(inner).astype(bf16)
        staged[block] = plain(act, w_out[...]).astype(bf16).reshape(nd, slots, width)

    exchange(ne, nd, rows_out, arrived, staged, halves, own_sums, returned, sems, work)
    logits = across(b, router[...])
    lane = lax.broadcasted_iota(jnp.int32, logits.shape, 1)
    logits = jnp.where(lane < ne, logits, -1e30)
    expo = jnp.exp(logits - jnp.max(logits, axis=-1, keepdims=True))
    share = expo / jnp.sum(expo, axis=-1, keepdims=True)
    shares[...] = share
    weight = jnp.sum(share * route_hot[...], axis=-1, keepdims=True)
    gate[...] = weight
    result = plain(sending_t[...], returned[...].reshape(ne * slots, width))
    combined[...] = result
    y[...] = (h + weight * result).astype(bf16)

    @pl.when(section == 0)
    def _():
        handed.start()
        handed.wait_send()


def offset_sums(score_grad):
    count = score_grad.shape[0]
    row = lax.broadcasted_iota(jnp.int32, score_grad.shape, 0)
    step = 1
    while step < count:
        moved = pltpu.roll(score_grad, count - step, 1)
        score_grad = jnp.where(lax.rem(row // step, 2) == 1, moved, score_grad)
        step *= 2
    return jnp.sum(score_grad, axis=0, keepdims=True)


def backward_kernel(
    ne, nd, size, summed,
    cot, qkv_w, out_w, gains, router, sending_t, route_hot, w_in, w_out,
    x, normed_a, qkv, probs, mixed, hidden, normed_b, shares, gate, combined, forward_rows, pre,
    grad_source, qkv_total, out_total, gains_total, router_total, table_total, in_grad, out_grad,
    incoming, handing, grad_qkv, small, rows_out, arrived, inner_grad, act, staged, halves, own_sums,
    returned, hand_sems, *more_refs,
):
    f32, bf16 = jnp.float32, jnp.bfloat16
    section = lax.axis_index("section")
    e, d = lax.axis_index("expert"), lax.axis_index("dp")
    partner = {"section": 1 - section}
    greet(near_peers(ne, nd) + [partner])
    count, width = x.shape
    slots = rows_out.shape[1]
    handed = remote(handing, incoming, hand_sems.at[0], hand_sems.at[1], partner)

    @pl.when(section == 1)
    def _():
        incoming[...] = jnp.zeros_like(incoming)

    @pl.when(section == 0)
    def _():
        handed.wait_recv()

    grad_out = cot[...].astype(f32) + incoming[...].astype(f32)
    grad_gate = jnp.sum(grad_out * combined[...], axis=-1, keepdims=True)
    grad_comb = (grad_out * gate[...]).astype(bf16)
    rows_out[...] = within(sending_t[...], grad_comb).astype(bf16).reshape(ne, slots, width)

    def work(pe):
        block = pl.ds(pe * nd, nd)
        rows = arrived[block].reshape(nd * slots, width)
        grad_act = across(rows, w_out[...])
        u = pre[block].reshape(nd * slots, -1)
        square = u * u
        bend = jnp.tanh(0.7978845608028654 * (u + 0.044715 * square * u))
        act[block] = (0.5 * u * (1.0 + bend)).astype(bf16).reshape(nd, slots, -1)
        slope = 0.5 * (1.0 + bend) + 0.5 * u * (1.0 - bend * bend) * (
            0.7978845608028654 * (1.0 + 3 * 0.044715 * square)
        )
        grad = (grad_act * slope).astype(bf16)
        inner_grad[block] = grad.reshape(nd, slots, -1)
        staged[block] = across(grad, w_in[...]).astype(bf16).reshape(nd, slots, width)

    exchange(
        ne, nd, rows_out, arrived, staged, halves, own_sums, returned, more_refs[:7], work
    )
    sum_refs = more_refs[7:]
    share = shares[...]
    grad_logits = (grad_gate * share * (route_hot[...] - gate[...])).astype(bf16)
    grad_normed = plain(sending_t[...], returned[...].reshape(ne * slots, width)) + plain(grad_logits, router[...])
    back, grad_gain_b = rms_back(grad_normed, hidden[...], gains[1:2, :])
    grad_hidden = back + grad_out
    grad_attn = grad_hidden.astype(bf16)
    grad_mixed = across(grad_attn, out_w[...]).astype(bf16)

    parts = sum_refs[0] if summed else None
    stage = Sums(ne, nd, sum_refs) if summed else None

    def part(c, left, right):
        value = within(left, right)
        if summed:
            parts[c] = value.astype(bf16).reshape((ne, nd) + parts.shape[3:])
            stage.send_first(c)
        else:
            (out_total if c == 3 else qkv_total.at[c])[...] = value

    part(3, mixed[...], grad_attn)
    masks = head_masks(count, size)
    offsets = []
    for pair in range(width // 128):
        lanes = slice(pair * 128, (pair + 1) * 128)
        q, k, v = qkv[0, :, lanes], qkv[1, :, lanes], qkv[2, :, lanes]
        grad_o = grad_mixed[:, lanes]
        grad_q = grad_k = grad_v = jnp.zeros((count, 128), f32)
        for i, mask in enumerate(masks):
            head = pair * len(masks) + i
            p = probs[head]
            own = only(mask, grad_o)
            grad_p = across(own, v)
            delta = jnp.sum(p * grad_p, axis=-1, keepdims=True)
            grad_s = (p * (grad_p - delta)).astype(bf16)
            grad_v = grad_v + within(p.astype(bf16), own)
            grad_q = grad_q + plain(grad_s, only(mask, k))
            grad_k = grad_k + within(grad_s, only(mask, q))
            offsets.append(offset_sums(grad_s.astype(f32)))
        grad_qkv[0, :, lanes] = (grad_q * (size**-0.5)).astype(bf16)
        grad_qkv[1, :, lanes] = (grad_k * (size**-0.5)).astype(bf16)
        grad_qkv[2, :, lanes] = grad_v.astype(bf16)
    grad_a = across(grad_qkv[0], qkv_w[0])
    for c in range(1, 3):
        grad_a = grad_a + across(grad_qkv[c], qkv_w[c])
    back, grad_gain_a = rms_back(grad_a, x[...].astype(f32), gains[0:1, :])
    grad_x = grad_hidden + back
    grad_source[...] = grad_x

    @pl.when(section == 1)
    def _():
        handing[...] = grad_x.astype(bf16)
        handed.start()

    for c in range(3):
        part(c, normed_a[...], grad_qkv[c])
    small[...] = jnp.zeros_like(small)
    small[0:1, :] = grad_gain_a
    small[1:2, :] = grad_gain_b
    small[8 : 8 + ne, :] = within(grad_logits, normed_b[...])[:ne]
    for head, value in enumerate(offsets):
        small[16 + head : 17 + head, :count] = value
    if summed:
        stage.small.send_first(small)
    rows = arrived.shape[0] * slots
    in_grad[...] = within(
        forward_rows[...].reshape(rows, width), inner_grad[...].reshape(rows, -1)
    )
    out_grad[...] = within(act[...].reshape(rows, -1), arrived[...].reshape(rows, width))
    if summed:
        for c in (3, 0, 1, 2):
            stage.send_second(c)
        stage.small.send_second()
        for c in (3, 0, 1, 2):
            (out_total if c == 3 else qkv_total.at[c])[...] = stage.finish(c)
        small_sum = stage.small.finish()
        piece = gains_total.shape[1]
        at = (e * nd + d) * piece
        mine = pltpu.roll(small_sum[:16], lax.rem(width - at, width), 1)
        gains_total[...] = mine[0:2, :piece]
        router_total[...] = mine[:, :128].T[:piece, 8 : 8 + ne]
        lane = lax.broadcasted_iota(jnp.int32, (BUCKETS, count), 1)
        bucket = bucket_of(jnp.where(lane < SEQ, lane, lane - count))
        hot = (bucket == lax.broadcasted_iota(jnp.int32, (BUCKETS, count), 0)).astype(f32)
        table_total[...] = lax.dot_general(
            hot, small_sum[16:, :count], (((1,), (1,)), ((), ())),
            precision=lax.Precision.HIGHEST, preferred_element_type=f32,
        )[:, : table_total.shape[1]]
        stage.wait_sent()
        stage.small.wait_sent()
    else:
        gains_total[...] = small[0:2, :]
        router_total[...] = small[8 : 8 + ne, :].T
        table_total[...] = jnp.zeros_like(table_total)
        for b in range(BUCKETS):
            lane = lax.broadcasted_iota(jnp.int32, (small.shape[0] - 16, count), 1)
            here = bucket_of(jnp.where(lane < SEQ, lane, lane - count)) == b
            sums = jnp.sum(jnp.where(here, small[16:, :count], 0.0), axis=1, keepdims=True)
            table_total[b : b + 1, :] = sums.T[:, : table_total.shape[1]]

    @pl.when(section == 1)
    def _():
        handed.wait_send()


def in_order(ref, count, pick):
    total = pick(ref, 0).astype(jnp.float32)
    for j in range(1, count):
        total = total + pick(ref, j).astype(jnp.float32)
    return total


class Sums:
    def __init__(self, ne, nd, refs):
        self.ne, self.nd = ne, nd
        self.e, self.d = lax.axis_index("expert"), lax.axis_index("dp")
        (
            self.parts, self.first, self.staged, self.second,
            self.send_a, self.recv_a, self.send_b, self.recv_b,
        ) = refs[:8]
        self.along_e = [lax.rem(self.e + k, ne) for k in range(1, ne)]
        self.along_d = [lax.rem(self.d + k, nd) for k in range(1, nd)]
        self.sent = []
        self.small = SmallSums(self, refs[8:])

    def send_first(self, c):
        for k, pd in enumerate(self.along_d):
            copy = remote(
                self.parts.at[c, :, pd], self.first.at[c, self.d],
                self.send_a.at[c, k], self.recv_a.at[c, self.d], at_group(self.e, pd),
            )
            copy.start()
            self.sent.append(copy)
        self.first[c, self.d] = self.parts[c, :, self.d]

    def send_second(self, c):
        for pd in self.along_d:
            remote(
                self.parts.at[c, :, pd], self.first.at[c, pd],
                self.send_a.at[c, 0], self.recv_a.at[c, pd], at_group(self.e, pd),
            ).wait_recv()
        total = in_order(self.first, self.nd, lambda ref, j: ref[c, j])
        self.staged[c] = total.astype(jnp.bfloat16)
        for k, pe in enumerate(self.along_e):
            copy = remote(
                self.staged.at[c, pe], self.second.at[c, self.e],
                self.send_b.at[c, k], self.recv_b.at[c, self.e], at_group(pe, self.d),
            )
            copy.start()
            self.sent.append(copy)
        self.second[c, self.e] = self.staged[c, self.e]

    def finish(self, c):
        for pe in self.along_e:
            remote(
                self.staged.at[c, pe], self.second.at[c, pe],
                self.send_b.at[c, 0], self.recv_b.at[c, pe], at_group(pe, self.d),
            ).wait_recv()
        return in_order(self.second, self.ne, lambda ref, j: ref[c, j])

    def wait_sent(self):
        for copy in self.sent:
            copy.wait_send()


class SmallSums:
    def __init__(self, outer, refs):
        self.outer = outer
        (
            self.mine, self.first, self.staged, self.second,
            self.send_a, self.recv_a, self.send_b, self.recv_b,
        ) = refs
        self.sent = []

    def spread(self, source, target, send, recv, peers, me):
        for k, peer in enumerate(peers):
            copy = remote(source, target.at[me], send.at[k], recv.at[me], peer)
            copy.start()
            self.sent.append(copy)
        target[me] = source[...]

    def arrive(self, source, target, send, recv, count, peers, slots):
        for peer, slot in zip(peers, slots):
            remote(source, target.at[slot], send.at[0], recv.at[slot], peer).wait_recv()
        return in_order(target, count, lambda ref, j: ref[j])

    def send_first(self, values):
        o = self.outer
        self.mine[...] = values[...].astype(jnp.bfloat16)
        self.peers_d = [at_group(o.e, pd) for pd in o.along_d]
        self.peers_e = [at_group(pe, o.d) for pe in o.along_e]
        self.spread(self.mine, self.first, self.send_a, self.recv_a, self.peers_d, o.d)

    def send_second(self):
        o = self.outer
        total = self.arrive(
            self.mine, self.first, self.send_a, self.recv_a, o.nd, self.peers_d, o.along_d
        )
        self.staged[...] = total.astype(jnp.bfloat16)
        self.spread(self.staged, self.second, self.send_b, self.recv_b, self.peers_e, o.e)

    def finish(self):
        o = self.outer
        return self.arrive(
            self.staged, self.second, self.send_b, self.recv_b, o.ne, self.peers_e, o.along_e
        )

    def wait_sent(self):
        for copy in self.sent:
            copy.wait_send()


def call(kernel, operands, outs, scratch, ident, name):
    vmem = pl.BlockSpec(memory_space=pltpu.VMEM)
    return pl.pallas_call(
        kernel,
        out_shape=[jax.ShapeDtypeStruct(shape, dtype) for shape, dtype in outs],
        in_specs=[vmem] * len(operands),
        out_specs=[vmem] * len(outs),
        scratch_shapes=scratch,
        compiler_params=pltpu.CompilerParams(
            collective_id=ident, has_side_effects=True, vmem_limit_bytes=VMEM_LIMIT
        ),
        name=name,
    )(*operands)


def on_device(
    tokens,
    cotangent,
    qkv_weight,
    out_weight,
    norm_gains,
    router_weight,
    bias_table,
    expert_in,
    expert_out,
    routes,
):
    f32, bf16 = jnp.float32, jnp.bfloat16
    ne, nd = lax.axis_size("expert"), lax.axis_size("dp")
    groups = ne * nd
    count, width = tokens.shape
    heads = bias_table.shape[2]
    size = width // heads
    capacity = max(2, SEQ * 4 // (3 * ne))
    per_device = count // SEQ
    slots = -(-per_device * capacity // 16) * 16
    piece = out_weight.shape[1]
    inner = expert_in.shape[3]
    lanes = 128
    dma = pltpu.SemaphoreType.DMA

    at = (lax.axis_index("expert") * nd + lax.axis_index("dp")) * piece
    small_shard = jnp.concatenate(
        [router_weight[0].T, jnp.zeros((8 - ne, piece), bf16), norm_gains[0]]
    )
    small_shard = lax.dynamic_update_slice(jnp.zeros((16, width), bf16), small_shard, (0, at))
    qkv_w, out_w, gains, router, bias, sending_t, route_hot = gather_shards(
        qkv_weight[0], out_weight, small_shard[None], bias_table[0].astype(f32), routes[0],
        ne, nd, capacity, slots, 0,
    )
    qkv_w = qkv_w.reshape(3, width, width)
    out_w = out_w.reshape(width, width)
    w_in, w_out = expert_in[0, 0], expert_out[0, 0]

    row, wide = (count, width), (groups, slots, width)
    deep = (groups, slots, inner)
    moe_sems = [
        dma((ne - 1,)), dma((ne, nd - 1)), dma((groups,)), dma((ne, nd - 1)), dma((groups,)),
        dma((ne - 1,)), dma((ne,)),
    ]
    back = (ne, slots, width)
    moe_rows = [
        pltpu.VMEM(wide, bf16), pltpu.VMEM(wide, bf16), pltpu.VMEM((ne - 1,) + back[1:], bf16),
        pltpu.VMEM(back, bf16),
    ]
    kept = call(
        partial(forward_kernel, ne, nd, size),
        (tokens, qkv_w, out_w, gains, router, bias, sending_t, route_hot, w_in, w_out),
        (
            (row, bf16), (row, bf16), ((3,) + row, bf16), ((heads, count, count), f32),
            (row, bf16), (row, f32), (row, bf16), ((count, lanes), f32), ((count, 1), f32),
            (row, f32), (wide, bf16), (deep, f32), (row, bf16),
        ),
        [
            pltpu.VMEM(back, bf16), *moe_rows, dma((2,)),
        ] + moe_sems,
        1, "forward_layers",
    )
    kept, output = kept[:-1], kept[-1]

    summed = piece % 16 == 0
    small_rows = 16 + -(-heads // 16) * 16
    scratch = [
        pltpu.VMEM(row, bf16), pltpu.VMEM(row, bf16), pltpu.VMEM((3,) + row, bf16),
        pltpu.VMEM((small_rows, width), f32),
        pltpu.VMEM((ne, slots, width), bf16), pltpu.VMEM(wide, bf16), pltpu.VMEM(deep, bf16),
        pltpu.VMEM(deep, bf16), *moe_rows, dma((2,)),
    ] + moe_sems
    if summed:
        tile = (piece, width)
        scratch += [
            pltpu.VMEM((4, ne, nd) + tile, bf16), pltpu.VMEM((4, nd, ne) + tile, bf16),
            pltpu.VMEM((4, ne) + tile, bf16), pltpu.VMEM((4, ne) + tile, bf16),
            dma((4, nd - 1)), dma((4, nd)), dma((4, ne - 1)), dma((4, ne)),
        ]
        tile = (small_rows, width)
        scratch += [
            pltpu.VMEM(tile, bf16), pltpu.VMEM((nd,) + tile, bf16), pltpu.VMEM(tile, bf16),
            pltpu.VMEM((ne,) + tile, bf16),
            dma((nd - 1,)), dma((nd,)), dma((ne - 1,)), dma((ne,)),
        ]
    part = piece if summed else width
    grad_source, *totals, in_grad, out_grad = call(
        partial(backward_kernel, ne, nd, size, summed),
        (
            cotangent[0], qkv_w, out_w, gains, router, sending_t, route_hot, w_in, w_out, *kept,
        ),
        (
            (row, f32), ((3, part, width), f32), ((part, width), f32), ((2, part), f32),
            ((part, ne), f32), ((BUCKETS, heads), f32), ((width, inner), f32),
            ((inner, width), f32),
        ),
        scratch, 2, "backward_layers",
    )
    if not summed:
        both = ("expert", "dp")
        dims = (1, 0, 1, 0)
        totals = [
            lax.psum_scatter(t, both, scatter_dimension=dim, tiled=True)
            for t, dim in zip(totals, dims)
        ] + [lax.psum(totals[4], both)]
    return (output[None], grad_source[None], *(t[None] for t in totals), in_grad[None, None],
            out_grad[None, None])


def solution(mesh):
    placed = (
        P(("expert", "dp"), None),
        P("section", ("expert", "dp"), None),
        P("section", None, ("expert", "dp"), None),
        P("section", ("expert", "dp"), None),
        P("section", None, ("expert", "dp")),
        P("section", ("expert", "dp"), None),
        P("section", None, None),
        P("section", "expert", None, "dp"),
        P("section", "expert", "dp", None),
        P("section", ("expert", "dp"), None),
    )
    return jax.shard_map(
        on_device,
        mesh=mesh,
        in_specs=placed,
        out_specs=(
            P("section", ("expert", "dp"), None),
            P("section", ("expert", "dp"), None),
            P("section", None, ("expert", "dp"), None),
            P("section", ("expert", "dp"), None),
            P("section", None, ("expert", "dp")),
            P("section", ("expert", "dp"), None),
            P("section", None, None),
            P("section", "expert", None, "dp"),
            P("section", "expert", "dp", None),
        ),
        check_vma=False,
    )
```

```python
from functools import partial

import jax
import jax.numpy as jnp
from jax import lax
from jax.experimental import pallas as pl
from jax.experimental.pallas import tpu as pltpu
from jax.sharding import PartitionSpec as P

BUCKETS = 32
SEQ = 64


EPSILON = 1e-06
BUCKET_EDGES = (12, 16, 23, 32, 46, 64, 91)


def gelu_tanh(values):
    return jax.nn.gelu(values, approximate=True)


MESH = pl.DeviceIdType.MESH
VMEM_LIMIT = 62 * 1024 * 1024


def at_group(e, d):
    return {"expert": e, "dp": d}


def greet(peers):
    barrier = pltpu.get_barrier_semaphore()
    for peer in peers:
        pl.semaphore_signal(barrier, inc=1, device_id=peer, device_id_type=MESH)
    pl.semaphore_wait(barrier, len(peers))


def remote(src, dst, send_sem, recv_sem, peer):
    return pltpu.make_async_remote_copy(
        src_ref=src, dst_ref=dst, send_sem=send_sem, recv_sem=recv_sem,
        device_id=peer, device_id_type=MESH,
    )


def near_peers(ne, nd):
    e, d = lax.axis_index("expert"), lax.axis_index("dp")
    return [at_group(lax.rem(e + k, ne), d) for k in range(1, ne)] + [
        at_group(e, lax.rem(d + k, nd)) for k in range(1, nd)
    ]


def bucket_of(offset):
    distance = jnp.abs(offset)
    far_bucket = 8 + sum(((distance >= edge).astype(jnp.int32) for edge in BUCKET_EDGES))
    near_far = jnp.where(distance < 8, distance, far_bucket)
    return near_far + 16 * (offset > 0).astype(jnp.int32)


def prepare(ne, capacity, table, route, bias, sending_t, route_hot):
    heads, count = bias.shape[:2]
    square = (count, count)
    query = lax.broadcasted_iota(jnp.int32, square, 0)
    key = lax.broadcasted_iota(jnp.int32, square, 1)
    together = query // SEQ == key // SEQ
    bucket = bucket_of(key - query)
    for head in range(heads):
        value = jnp.full(square, -1e30, jnp.float32)
        for b in range(BUCKETS):
            value = jnp.where(bucket == b, table[b, head], value)
        bias[head] = jnp.where(together, value, -1e30)
    now = route[...]
    hot = now == lax.broadcasted_iota(jnp.int32, route_hot.shape, 1)
    route_hot[...] = hot.astype(jnp.float32)
    earlier = (together & (key < query)).astype(jnp.bfloat16)
    before = jnp.dot(earlier, hot.astype(jnp.bfloat16), preferred_element_type=jnp.float32)
    place = jnp.sum(jnp.where(hot, before, 0.0), axis=-1, keepdims=True).astype(jnp.int32)
    place = place + capacity * (lax.broadcasted_iota(jnp.int32, now.shape, 0) // SEQ)
    cell = now * (sending_t.shape[1] // ne) + place
    sending_t[...] = (
        cell == lax.broadcasted_iota(jnp.int32, sending_t.shape, 1)
    ).astype(jnp.float32).astype(jnp.bfloat16)


def enter(ne, nd, section, partner, ready):
    barrier = pltpu.get_barrier_semaphore()
    peers = near_peers(ne, nd)
    for peer in peers:
        pl.semaphore_signal(barrier, inc=1, device_id=peer, device_id_type=MESH)

    @pl.when(section == 0)
    def _():
        pl.semaphore_signal(barrier, inc=1, device_id=partner, device_id_type=MESH)
        pl.semaphore_wait(barrier, len(peers))

    @pl.when(section == 1)
    def _():
        pl.semaphore_wait(barrier, len(peers) + 1)
        pl.semaphore_signal(ready, inc=1, device_id=partner, device_id_type=MESH)


def gather_kernel(
    ne, nd, capacity,
    qkv_shard, out_shard, small_shard, table, route,
    qkv_full, out_full, gains, router, bias, sending_t, route_hot,
    small_full, send_sem, recv_sem, own_sem, turn_sem,
):
    count = 3
    shards, fulls = (qkv_shard, out_shard, small_shard), (qkv_full, out_full, small_full)
    section = lax.axis_index("section")
    partner = {"section": 1 - section}
    e, d = lax.axis_index("expert"), lax.axis_index("dp")
    along_e = [lax.rem(e + k, ne) for k in range(1, ne)]
    along_d = [lax.rem(d + k, nd) for k in range(1, nd)]
    greet(near_peers(ne, nd) + [partner])

    @pl.when(section == 1)
    def _():
        prepare(ne, capacity, table, route, bias, sending_t, route_hot)
        pl.semaphore_wait(turn_sem, 1)

    me = e * nd + d
    waits = []
    for i in range(count):
        own = pltpu.make_async_copy(shards[i], fulls[i].at[:, me], own_sem.at[i])
        own.start()
        waits.append(own.wait)

    def send(i, slot, source, step, peer):
        copy = remote(
            source, fulls[i].at[:, slot], send_sem.at[i, step], recv_sem.at[i, slot], peer
        )
        copy.start()
        waits.append(copy.wait_send)

    def arrive(i, slot, peer):
        remote(
            fulls[i].at[:, slot], fulls[i].at[:, slot], send_sem.at[i, 0], recv_sem.at[i, slot], peer
        ).wait_recv()

    for i in range(count):
        for k, pe in enumerate(along_e):
            send(i, me, shards[i], k, at_group(pe, d))
    for i in range(count):
        for k, pd in enumerate(along_d):
            send(i, me, shards[i], ne - 1 + k, at_group(e, pd))
    @pl.when(section == 0)
    def _():
        prepare(ne, capacity, table, route, bias, sending_t, route_hot)

    for j, pe in enumerate(along_e):
        slot = pe * nd + d
        for i in range(count):
            arrive(i, slot, at_group(pe, d))
            for k, pd in enumerate(along_d):
                step = ne - 1 + (j + 1) * (nd - 1) + k
                send(i, slot, fulls[i].at[:, slot], step, at_group(e, pd))
    for ke in range(ne):
        for pd in along_d:
            for i in range(count):
                arrive(i, lax.rem(e + ke, ne) * nd + pd, at_group(e, pd))

    @pl.when(section == 0)
    def _():
        pl.semaphore_signal(turn_sem, inc=1, device_id=partner, device_id_type=MESH)

    for wait in waits:
        wait()
    small = in_order(small_full, ne * nd, lambda ref, g: ref[0, g])
    gains[...] = small[8:10]
    router[...] = jnp.zeros_like(router)
    router[0:16, :] = jnp.where(
        lax.broadcasted_iota(jnp.int32, small.shape, 0) < ne, small, 0.0
    ).astype(router.dtype)


def gather_shards(qkv, out, small, table, route, ne, nd, capacity, slots, ident):
    groups = ne * nd
    count, width, heads, lanes = route.shape[0], small.shape[2], table.shape[1], 128
    anywhere = pl.BlockSpec(memory_space=pl.ANY)
    vmem = pl.BlockSpec(memory_space=pltpu.VMEM)
    dma = pltpu.SemaphoreType.DMA
    f32, bf16 = jnp.float32, jnp.bfloat16
    outs = (
        ((3, groups) + qkv.shape[1:], bf16), ((1, groups) + out.shape[1:], bf16),
        ((2, width), f32), ((lanes, width), bf16), ((heads, count, count), f32),
        ((count, ne * slots), bf16), ((count, lanes), f32),
    )
    return pl.pallas_call(
        partial(gather_kernel, ne, nd, capacity),
        out_shape=[jax.ShapeDtypeStruct(shape, dtype) for shape, dtype in outs],
        in_specs=[anywhere, anywhere, vmem, pl.BlockSpec(memory_space=pltpu.SMEM), vmem],
        out_specs=[anywhere] * 2 + [vmem] * 5,
        scratch_shapes=[
            pltpu.VMEM((1, groups) + small.shape[1:], bf16),
            dma((3, ne - 1 + ne * (nd - 1))), dma((3, groups)), dma((3,)),
            pltpu.SemaphoreType.REGULAR,
        ],
        compiler_params=pltpu.CompilerParams(
            collective_id=ident, has_side_effects=True, vmem_limit_bytes=VMEM_LIMIT
        ),
        name="gather_weights",
    )(qkv, out, small, table, route)


def exchange(ne, nd, rows_out, arrived, staged, halves, summed, returned, sems, work):
    send_e, send_d, recv_a, send_p, recv_p, send_b, recv_b = sems
    e, d = lax.axis_index("expert"), lax.axis_index("dp")
    me = e * nd + d
    order = [lax.rem(e + ne - k, ne) for k in range(ne)]
    along_d = [lax.rem(d + k, nd) for k in range(1, nd)]
    waits = []

    def start(copy):
        copy.start()
        waits.append(copy.wait_send)

    for k in range(1, ne):
        pe = lax.rem(e + k, ne)
        start(remote(
            rows_out.at[pe], arrived.at[me], send_e.at[k - 1], recv_a.at[me], at_group(pe, d)
        ))
    for j, pd in enumerate(along_d):
        start(remote(
            rows_out.at[e], arrived.at[me], send_d.at[0, j], recv_a.at[me], at_group(e, pd)
        ))
    arrived[me] = rows_out[e]

    def forward(k):
        slot = order[k] * nd + d
        remote(
            arrived.at[slot], arrived.at[slot], send_e.at[0], recv_a.at[slot],
            at_group(order[k], d),
        ).wait_recv()
        for j, pd in enumerate(along_d):
            start(remote(
                arrived.at[slot], arrived.at[slot], send_d.at[k, j], recv_a.at[slot],
                at_group(e, pd),
            ))

    def step(k):
        pe = order[k]
        for pd in along_d:
            slot = pe * nd + pd
            remote(
                arrived.at[slot], arrived.at[slot], send_d.at[k, 0], recv_a.at[slot],
                at_group(e, pd),
            ).wait_recv()
        work(pe)
        for j, pd in enumerate(along_d):
            start(remote(
                staged.at[pe * nd + pd], halves.at[pe * nd + d], send_p.at[k, j],
                recv_p.at[pe * nd + d], at_group(e, pd),
            ))
        halves[pe * nd + d] = staged[pe * nd + d]

    def finish(k):
        pe = order[k]
        for pd in along_d:
            slot = pe * nd + pd
            remote(
                staged.at[slot], halves.at[slot], send_p.at[k, 0], recv_p.at[slot],
                at_group(e, pd),
            ).wait_recv()
        total = in_order(halves, nd, lambda ref, j: ref[pe * nd + j]).astype(jnp.bfloat16)
        if k:
            summed[k - 1] = total
            start(remote(
                summed.at[k - 1], returned.at[e], send_b.at[k - 1], recv_b.at[e], at_group(pe, d)
            ))
        else:
            returned[e] = total

    for k in range(1, ne):
        forward(k)
        if k == 1:
            step(0)
    for k in range(1, ne):
        step(k)
        if k > 1:
            finish(k - 1)
    finish(ne - 1)
    finish(0)
    for pe in order[1:]:
        remote(
            summed.at[0], returned.at[pe], send_b.at[0], recv_b.at[pe], at_group(pe, d)
        ).wait_recv()
    for wait in waits:
        wait()


def across(left, right):
    return lax.dot_general(
        left, right, (((1,), (1,)), ((), ())), preferred_element_type=jnp.float32
    )


def within(left, right):
    return lax.dot_general(
        left, right, (((0,), (0,)), ((), ())), preferred_element_type=jnp.float32
    )


def plain(left, right):
    return jnp.dot(left, right, preferred_element_type=jnp.float32)


def inverse_rms(values):
    return lax.rsqrt(jnp.mean(values * values, axis=-1, keepdims=True) + EPSILON)


def rms_back(grad, values, gain):
    scale = inverse_rms(values)
    turned = grad * gain
    inner = jnp.mean(turned * values, axis=-1, keepdims=True)
    back = scale * turned - values * (scale * scale * scale * inner)
    return back, jnp.sum(grad * values * scale, axis=0, keepdims=True)


def head_masks(count, size):
    lane = lax.broadcasted_iota(jnp.int32, (count, 128), 1)
    return [(lane >= i * size) & (lane < (i + 1) * size) for i in range(128 // size)]


def only(mask, values):
    return jnp.where(mask, values, jnp.zeros_like(values))


def forward_kernel(
    ne, nd, size,
    tokens, qkv_w, out_w, gains, router, bias, sending_t, route_hot, w_in, w_out,
    x, normed_a, qkv, probs, mixed, hidden, normed_b, shares, gate, combined, arrived, pre, y,
    rows_out, staged, halves, own_sums, returned, hand_sems, ready, *sems,
):
    f32, bf16 = jnp.float32, jnp.bfloat16
    section = lax.axis_index("section")
    partner = {"section": 1 - section}
    enter(ne, nd, section, partner, ready)
    count, width = x.shape
    slots = rows_out.shape[1]
    handed = remote(y, x, hand_sems.at[0], hand_sems.at[1], partner)

    @pl.when(section == 0)
    def _():
        x[...] = tokens[...]

    @pl.when(section == 1)
    def _():
        handed.wait_recv()

    source = x[...].astype(f32)
    a = (source * inverse_rms(source) * gains[0:1, :]).astype(bf16)
    normed_a[...] = a
    for c in range(3):
        qkv[c] = plain(a, qkv_w[c]).astype(bf16)
    masks = head_masks(count, size)
    for pair in range(width // 128):
        lanes = pl.ds(pair * 128, 128)
        q, k, v = qkv[0, :, lanes], qkv[1, :, lanes], qkv[2, :, lanes]
        joined = jnp.zeros((count, 128), f32)
        for i, mask in enumerate(masks):
            head = pair * len(masks) + i
            score = across(only(mask, q), k) * (size**-0.5) + bias[head]
            expo = jnp.exp(score - jnp.max(score, axis=-1, keepdims=True))
            p = expo / jnp.sum(expo, axis=-1, keepdims=True)
            probs[head] = p
            joined = jnp.where(mask, plain(p.astype(bf16), v), joined)
        mixed[:, lanes] = joined.astype(bf16)
    h = source + plain(mixed[...], out_w[...])
    hidden[...] = h
    b = (h * inverse_rms(h) * gains[1:2, :]).astype(bf16)
    normed_b[...] = b
    rows_out[...] = within(sending_t[...], b).astype(bf16).reshape(ne, slots, width)

    def work(pe):
        block = pl.ds(pe * nd, nd)
        rows = arrived[block].reshape(nd * slots, width)
        inner = plain(rows, w_in[...])
        pre[block] = inner.reshape(nd, slots, -1)
        act = gelu_tanh(inner).astype(bf16)
        staged[block] = plain(act, w_out[...]).astype(bf16).reshape(nd, slots, width)

    exchange(ne, nd, rows_out, arrived, staged, halves, own_sums, returned, sems, work)
    logits = across(b, router[...])
    lane = lax.broadcasted_iota(jnp.int32, logits.shape, 1)
    logits = jnp.where(lane < ne, logits, -1e30)
    expo = jnp.exp(logits - jnp.max(logits, axis=-1, keepdims=True))
    share = expo / jnp.sum(expo, axis=-1, keepdims=True)
    shares[...] = share
    weight = jnp.sum(share * route_hot[...], axis=-1, keepdims=True)
    gate[...] = weight
    result = plain(sending_t[...], returned[...].reshape(ne * slots, width))
    combined[...] = result
    y[...] = (h + weight * result).astype(bf16)

    @pl.when(section == 0)
    def _():
        pl.semaphore_wait(ready, 1)
        handed.start()
        handed.wait_send()


def offset_sums(score_grad):
    count = score_grad.shape[0]
    row = lax.broadcasted_iota(jnp.int32, score_grad.shape, 0)
    step = 1
    while step < count:
        moved = pltpu.roll(score_grad, count - step, 1)
        score_grad = jnp.where(lax.rem(row // step, 2) == 1, moved, score_grad)
        step *= 2
    return jnp.sum(score_grad, axis=0, keepdims=True)


def backward_kernel(
    ne, nd, size, summed, entered,
    cot, qkv_w, out_w, gains, router, sending_t, route_hot, w_in, w_out,
    x, normed_a, qkv, probs, mixed, hidden, normed_b, shares, gate, combined, forward_rows, pre,
    grad_source, qkv_total, out_total, gains_total, router_total, table_total, in_grad, out_grad,
    incoming, handing, grad_qkv, score_grads, small, rows_out, arrived, inner_grad, act, staged, halves, own_sums,
    returned, hand_sems, *more_refs,
):
    f32, bf16 = jnp.float32, jnp.bfloat16
    section = lax.axis_index("section")
    e, d = lax.axis_index("expert"), lax.axis_index("dp")
    partner = {"section": 1 - section}
    if not entered:
        greet(near_peers(ne, nd) + [partner])
    count, width = x.shape
    slots = rows_out.shape[1]
    handed = remote(handing, incoming, hand_sems.at[0], hand_sems.at[1], partner)

    @pl.when(section == 1)
    def _():
        incoming[...] = jnp.zeros_like(incoming)

    @pl.when(section == 0)
    def _():
        handed.wait_recv()

    grad_out = cot[...].astype(f32) + incoming[...].astype(f32)
    grad_gate = jnp.sum(grad_out * combined[...], axis=-1, keepdims=True)
    grad_comb = (grad_out * gate[...]).astype(bf16)
    rows_out[...] = within(sending_t[...], grad_comb).astype(bf16).reshape(ne, slots, width)

    def work(pe):
        block = pl.ds(pe * nd, nd)
        rows = arrived[block].reshape(nd * slots, width)
        grad_act = across(rows, w_out[...])
        u = pre[block].reshape(nd * slots, -1)
        square = u * u
        bend = jnp.tanh(0.7978845608028654 * (u + 0.044715 * square * u))
        act[block] = (0.5 * u * (1.0 + bend)).astype(bf16).reshape(nd, slots, -1)
        slope = 0.5 * (1.0 + bend) + 0.5 * u * (1.0 - bend * bend) * (
            0.7978845608028654 * (1.0 + 3 * 0.044715 * square)
        )
        grad = (grad_act * slope).astype(bf16)
        inner_grad[block] = grad.reshape(nd, slots, -1)
        staged[block] = across(grad, w_in[...]).astype(bf16).reshape(nd, slots, width)

    exchange(
        ne, nd, rows_out, arrived, staged, halves, own_sums, returned, more_refs[:7], work
    )
    sum_refs = more_refs[7:]
    share = shares[...]
    grad_logits = (grad_gate * share * (route_hot[...] - gate[...])).astype(bf16)
    grad_normed = plain(sending_t[...], returned[...].reshape(ne * slots, width)) + plain(grad_logits, router[...])
    back, grad_gain_b = rms_back(grad_normed, hidden[...], gains[1:2, :])
    grad_hidden = back + grad_out
    grad_attn = grad_hidden.astype(bf16)
    grad_mixed = across(grad_attn, out_w[...]).astype(bf16)

    parts = sum_refs[0] if summed else None
    stage = Sums(ne, nd, sum_refs) if summed else None

    def part(c, left, right):
        value = within(left, right)
        if summed:
            parts[c] = value.astype(bf16).reshape((ne, nd) + parts.shape[3:])
            stage.send_first(c)
        else:
            (out_total if c == 3 else qkv_total.at[c])[...] = value

    part(3, mixed[...], grad_attn)
    masks = head_masks(count, size)
    for pair in range(width // 128):
        lanes = slice(pair * 128, (pair + 1) * 128)
        q, k, v = qkv[0, :, lanes], qkv[1, :, lanes], qkv[2, :, lanes]
        grad_o = grad_mixed[:, lanes]
        grad_q = grad_k = grad_v = jnp.zeros((count, 128), f32)
        for i, mask in enumerate(masks):
            head = pair * len(masks) + i
            p = probs[head]
            own = only(mask, grad_o)
            grad_p = across(own, v)
            delta = jnp.sum(p * grad_p, axis=-1, keepdims=True)
            grad_s = (p * (grad_p - delta)).astype(bf16)
            grad_v = grad_v + within(p.astype(bf16), own)
            grad_q = grad_q + plain(grad_s, only(mask, k))
            grad_k = grad_k + within(grad_s, only(mask, q))
            score_grads[head] = grad_s
        grad_qkv[0, :, lanes] = (grad_q * (size**-0.5)).astype(bf16)
        grad_qkv[1, :, lanes] = (grad_k * (size**-0.5)).astype(bf16)
        grad_qkv[2, :, lanes] = grad_v.astype(bf16)
    grad_a = across(grad_qkv[0], qkv_w[0])
    for c in range(1, 3):
        grad_a = grad_a + across(grad_qkv[c], qkv_w[c])
    back, grad_gain_a = rms_back(grad_a, x[...].astype(f32), gains[0:1, :])
    grad_x = grad_hidden + back
    grad_source[...] = grad_x

    @pl.when(section == 1)
    def _():
        handing[...] = grad_x.astype(bf16)
        handed.start()

    for c in range(3):
        part(c, normed_a[...], grad_qkv[c])
    small[...] = jnp.zeros_like(small)
    small[0:1, :] = grad_gain_a
    small[1:2, :] = grad_gain_b
    small[8 : 8 + ne, :] = within(grad_logits, normed_b[...])[:ne]
    for head in range(probs.shape[0]):
        small[16 + head : 17 + head, :count] = offset_sums(score_grads[head].astype(f32))
    if summed:
        stage.small.send_first(small)
    rows = arrived.shape[0] * slots
    in_grad[...] = within(
        forward_rows[...].reshape(rows, width), inner_grad[...].reshape(rows, -1)
    )
    out_grad[...] = within(act[...].reshape(rows, -1), arrived[...].reshape(rows, width))
    if summed:
        for c in (3, 0, 1, 2):
            stage.send_second(c)
        stage.small.send_second()
        for c in (3, 0, 1, 2):
            (out_total if c == 3 else qkv_total.at[c])[...] = stage.finish(c)
        small_sum = stage.small.finish()
        piece = gains_total.shape[1]
        at = (e * nd + d) * piece
        mine = pltpu.roll(small_sum[:16], lax.rem(width - at, width), 1)
        gains_total[...] = mine[0:2, :piece]
        router_total[...] = mine[:, :128].T[:piece, 8 : 8 + ne]
        lane = lax.broadcasted_iota(jnp.int32, (BUCKETS, count), 1)
        bucket = bucket_of(jnp.where(lane < SEQ, lane, lane - count))
        hot = (bucket == lax.broadcasted_iota(jnp.int32, (BUCKETS, count), 0)).astype(f32)
        table_total[...] = lax.dot_general(
            hot, small_sum[16:, :count], (((1,), (1,)), ((), ())),
            precision=lax.Precision.HIGHEST, preferred_element_type=f32,
        )[:, : table_total.shape[1]]
        stage.wait_sent()
        stage.small.wait_sent()
    else:
        gains_total[...] = small[0:2, :]
        router_total[...] = small[8 : 8 + ne, :].T
        table_total[...] = jnp.zeros_like(table_total)
        for b in range(BUCKETS):
            lane = lax.broadcasted_iota(jnp.int32, (small.shape[0] - 16, count), 1)
            here = bucket_of(jnp.where(lane < SEQ, lane, lane - count)) == b
            sums = jnp.sum(jnp.where(here, small[16:, :count], 0.0), axis=1, keepdims=True)
            table_total[b : b + 1, :] = sums.T[:, : table_total.shape[1]]

    @pl.when(section == 1)
    def _():
        handed.wait_send()


def both_kernel(ne, nd, size, tokens, cot, *refs):
    weights, refs = refs[:9], refs[9:]
    qkv_w, out_w, gains, router, bias, sending_t, route_hot, w_in, w_out = weights
    y, outs, refs = refs[0], refs[1:9], refs[9:]
    kept, refs = refs[:12], refs[12:]
    forward_kernel(ne, nd, size, tokens, *weights, *kept, y, *refs[:14])
    backward_kernel(
        ne, nd, size, True, True, cot, qkv_w, out_w, gains, router, sending_t, route_hot, w_in,
        w_out, *kept, *outs, *refs[14:],
    )


def in_order(ref, count, pick):
    total = pick(ref, 0).astype(jnp.float32)
    for j in range(1, count):
        total = total + pick(ref, j).astype(jnp.float32)
    return total


class Sums:
    def __init__(self, ne, nd, refs):
        self.ne, self.nd = ne, nd
        self.e, self.d = lax.axis_index("expert"), lax.axis_index("dp")
        (
            self.parts, self.first, self.staged, self.second,
            self.send_a, self.recv_a, self.send_b, self.recv_b,
        ) = refs[:8]
        self.along_e = [lax.rem(self.e + k, ne) for k in range(1, ne)]
        self.along_d = [lax.rem(self.d + k, nd) for k in range(1, nd)]
        self.sent = []
        self.small = SmallSums(self, refs[8:])

    def send_first(self, c):
        for k, pd in enumerate(self.along_d):
            copy = remote(
                self.parts.at[c, :, pd], self.first.at[c, self.d],
                self.send_a.at[c, k], self.recv_a.at[c, self.d], at_group(self.e, pd),
            )
            copy.start()
            self.sent.append(copy)
        self.first[c, self.d] = self.parts[c, :, self.d]

    def send_second(self, c):
        for pd in self.along_d:
            remote(
                self.parts.at[c, :, pd], self.first.at[c, pd],
                self.send_a.at[c, 0], self.recv_a.at[c, pd], at_group(self.e, pd),
            ).wait_recv()
        total = in_order(self.first, self.nd, lambda ref, j: ref[c, j])
        self.staged[c] = total.astype(jnp.bfloat16)
        for k, pe in enumerate(self.along_e):
            copy = remote(
                self.staged.at[c, pe], self.second.at[c, self.e],
                self.send_b.at[c, k], self.recv_b.at[c, self.e], at_group(pe, self.d),
            )
            copy.start()
            self.sent.append(copy)
        self.second[c, self.e] = self.staged[c, self.e]

    def finish(self, c):
        for pe in self.along_e:
            remote(
                self.staged.at[c, pe], self.second.at[c, pe],
                self.send_b.at[c, 0], self.recv_b.at[c, pe], at_group(pe, self.d),
            ).wait_recv()
        return in_order(self.second, self.ne, lambda ref, j: ref[c, j])

    def wait_sent(self):
        for copy in self.sent:
            copy.wait_send()


class SmallSums:
    def __init__(self, outer, refs):
        self.outer = outer
        (
            self.mine, self.first, self.staged, self.second,
            self.send_a, self.recv_a, self.send_b, self.recv_b,
        ) = refs
        self.sent = []

    def spread(self, source, target, send, recv, peers, me):
        for k, peer in enumerate(peers):
            copy = remote(source, target.at[me], send.at[k], recv.at[me], peer)
            copy.start()
            self.sent.append(copy)
        target[me] = source[...]

    def arrive(self, source, target, send, recv, count, peers, slots):
        for peer, slot in zip(peers, slots):
            remote(source, target.at[slot], send.at[0], recv.at[slot], peer).wait_recv()
        return in_order(target, count, lambda ref, j: ref[j])

    def send_first(self, values):
        o = self.outer
        self.mine[...] = values[...].astype(jnp.bfloat16)
        self.peers_d = [at_group(o.e, pd) for pd in o.along_d]
        self.peers_e = [at_group(pe, o.d) for pe in o.along_e]
        self.spread(self.mine, self.first, self.send_a, self.recv_a, self.peers_d, o.d)

    def send_second(self):
        o = self.outer
        total = self.arrive(
            self.mine, self.first, self.send_a, self.recv_a, o.nd, self.peers_d, o.along_d
        )
        self.staged[...] = total.astype(jnp.bfloat16)
        self.spread(self.staged, self.second, self.send_b, self.recv_b, self.peers_e, o.e)

    def finish(self):
        o = self.outer
        return self.arrive(
            self.staged, self.second, self.send_b, self.recv_b, o.ne, self.peers_e, o.along_e
        )

    def wait_sent(self):
        for copy in self.sent:
            copy.wait_send()


def call(kernel, operands, outs, scratch, ident, name):
    vmem = pl.BlockSpec(memory_space=pltpu.VMEM)
    return pl.pallas_call(
        kernel,
        out_shape=[jax.ShapeDtypeStruct(shape, dtype) for shape, dtype in outs],
        in_specs=[vmem] * len(operands),
        out_specs=[vmem] * len(outs),
        scratch_shapes=scratch,
        compiler_params=pltpu.CompilerParams(
            collective_id=ident, has_side_effects=True, vmem_limit_bytes=VMEM_LIMIT
        ),
        name=name,
    )(*operands)


def publish_kernel(*refs):
    half = (len(refs) - 1) // 2
    copies = [
        pltpu.make_async_copy(refs[i], refs[half + i], refs[-1].at[i]) for i in range(half)
    ]
    for copy in copies:
        copy.start()
    for copy in copies:
        copy.wait()


def publish(arrays):
    anywhere = pl.BlockSpec(memory_space=pl.ANY)
    return pl.pallas_call(
        publish_kernel,
        out_shape=[jax.ShapeDtypeStruct(a.shape, a.dtype) for a in arrays],
        in_specs=[anywhere] * len(arrays),
        out_specs=[anywhere] * len(arrays),
        scratch_shapes=[pltpu.SemaphoreType.DMA((len(arrays),))],
        name="publish",
    )(*arrays)


def on_device(
    tokens,
    cotangent,
    qkv_weight,
    out_weight,
    norm_gains,
    router_weight,
    bias_table,
    expert_in,
    expert_out,
    routes,
):
    f32, bf16 = jnp.float32, jnp.bfloat16
    ne, nd = lax.axis_size("expert"), lax.axis_size("dp")
    groups = ne * nd
    count, width = tokens.shape
    heads = bias_table.shape[2]
    size = width // heads
    capacity = max(2, SEQ * 4 // (3 * ne))
    per_device = count // SEQ
    slots = -(-per_device * capacity // 16) * 16
    piece = out_weight.shape[1]
    inner = expert_in.shape[3]
    lanes = 128
    dma = pltpu.SemaphoreType.DMA

    at = (lax.axis_index("expert") * nd + lax.axis_index("dp")) * piece
    small_shard = jnp.concatenate(
        [router_weight[0].T, jnp.zeros((8 - ne, piece), bf16), norm_gains[0]]
    )
    small_shard = lax.dynamic_update_slice(jnp.zeros((16, width), bf16), small_shard, (0, at))
    qkv_w, out_w, gains, router, bias, sending_t, route_hot = gather_shards(
        qkv_weight[0], out_weight, small_shard[None], bias_table[0].astype(f32), routes[0],
        ne, nd, capacity, slots, 0,
    )
    qkv_w = qkv_w.reshape(3, width, width)
    out_w = out_w.reshape(width, width)
    w_in, w_out = expert_in[0, 0], expert_out[0, 0]

    row, wide = (count, width), (groups, slots, width)
    deep = (groups, slots, inner)
    moe_sems = [
        dma((ne - 1,)), dma((ne, nd - 1)), dma((groups,)), dma((ne, nd - 1)), dma((groups,)),
        dma((ne - 1,)), dma((ne,)),
    ]
    back = (ne, slots, width)
    moe_rows = [
        pltpu.VMEM(wide, bf16), pltpu.VMEM(wide, bf16), pltpu.VMEM((ne - 1,) + back[1:], bf16),
        pltpu.VMEM(back, bf16),
    ]
    kept_outs = (
            (row, bf16), (row, bf16), ((3,) + row, bf16), ((heads, count, count), f32),
            (row, bf16), (row, f32), (row, bf16), ((count, lanes), f32), ((count, 1), f32),
            (row, f32), (wide, bf16), (deep, f32), (row, bf16),
        )
    forward_scratch = [
            pltpu.VMEM(back, bf16), *moe_rows, dma((2,)), pltpu.SemaphoreType.REGULAR,
        ] + moe_sems
    summed = piece % 16 == 0
    small_rows = 16 + -(-heads // 16) * 16
    scratch = [
        pltpu.VMEM(row, bf16), pltpu.VMEM(row, bf16), pltpu.VMEM((3,) + row, bf16),
        pltpu.VMEM((heads, count, count), bf16), pltpu.VMEM((small_rows, width), f32),
        pltpu.VMEM((ne, slots, width), bf16), pltpu.VMEM(wide, bf16), pltpu.VMEM(deep, bf16),
        pltpu.VMEM(deep, bf16), *moe_rows, dma((2,)),
    ] + moe_sems
    if summed:
        tile = (piece, width)
        scratch += [
            pltpu.VMEM((4, ne, nd) + tile, bf16), pltpu.VMEM((4, nd, ne) + tile, bf16),
            pltpu.VMEM((4, ne) + tile, bf16), pltpu.VMEM((4, ne) + tile, bf16),
            dma((4, nd - 1)), dma((4, nd)), dma((4, ne - 1)), dma((4, ne)),
        ]
        tile = (small_rows, width)
        scratch += [
            pltpu.VMEM(tile, bf16), pltpu.VMEM((nd,) + tile, bf16), pltpu.VMEM(tile, bf16),
            pltpu.VMEM((ne,) + tile, bf16),
            dma((nd - 1,)), dma((nd,)), dma((ne - 1,)), dma((ne,)),
        ]
    part = piece if summed else width
    backward_outs = (
        (row, f32), ((3, part, width), f32), ((part, width), f32), ((2, part), f32),
        ((part, ne), f32), ((BUCKETS, heads), f32), ((width, inner), f32), ((inner, width), f32),
    )
    weights = (qkv_w, out_w, gains, router, bias, sending_t, route_hot, w_in, w_out)
    if summed:
        output, grad_source, *totals, in_grad, out_grad = call(
            partial(both_kernel, ne, nd, size),
            (tokens, cotangent[0], *weights),
            ((row, bf16),) + backward_outs,
            [pltpu.VMEM(shape, dtype) for shape, dtype in kept_outs[:-1]]
            + forward_scratch + scratch,
            1, "both_ways",
        )
    else:
        *kept, output = call(
            partial(forward_kernel, ne, nd, size), (tokens, *weights), kept_outs,
            forward_scratch, 1, "forward_layers",
        )
        grad_source, *totals, in_grad, out_grad = call(
            partial(backward_kernel, ne, nd, size, summed, False),
            (cotangent[0], *weights[:4], *weights[5:], *kept),
            backward_outs, scratch, 2, "backward_layers",
        )
    if not summed:
        both = ("expert", "dp")
        dims = (1, 0, 1, 0)
        totals = [
            lax.psum_scatter(t, both, scatter_dimension=dim, tiled=True)
            for t, dim in zip(totals, dims)
        ] + [lax.psum(totals[4], both)]
    output, grad_source, qkv_total, out_total, in_grad, out_grad = publish(
        (output, grad_source, totals[0], totals[1], in_grad, out_grad)
    )
    totals = [qkv_total, out_total] + list(totals[2:])
    return (output[None], grad_source[None], *(t[None] for t in totals), in_grad[None, None],
            out_grad[None, None])


def solution(mesh):
    placed = (
        P(("expert", "dp"), None),
        P("section", ("expert", "dp"), None),
        P("section", None, ("expert", "dp"), None),
        P("section", ("expert", "dp"), None),
        P("section", None, ("expert", "dp")),
        P("section", ("expert", "dp"), None),
        P("section", None, None),
        P("section", "expert", None, "dp"),
        P("section", "expert", "dp", None),
        P("section", ("expert", "dp"), None),
    )
    return jax.shard_map(
        on_device,
        mesh=mesh,
        in_specs=placed,
        out_specs=(
            P("section", ("expert", "dp"), None),
            P("section", ("expert", "dp"), None),
            P("section", None, ("expert", "dp"), None),
            P("section", ("expert", "dp"), None),
            P("section", None, ("expert", "dp")),
            P("section", ("expert", "dp"), None),
            P("section", None, None),
            P("section", "expert", None, "dp"),
            P("section", "expert", "dp", None),
        ),
        check_vma=False,
    )
```
